32 devices in a mesh: tm: 2 (over y), wall: 4 (over x, core), span: 4 (over z).
Axes of the slice: x: 2, y: 2, z: 4, core: 2. Of those that a mesh axis runs over, the one named last changes fastest.
Arguments:
- starting_speed_vector: float32 [3, 2, 16, 128, 512], P(None, 'tm', None, 'wall', 'span'), may hold values from -6 to 6
- driving_source: float32 [3, 2, 16, 128, 512], P(None, 'tm', None, 'wall', 'span'), may hold values from -3 to 3
- viscosity: float32 [128], P('wall'), may hold values from 0.02 to 0.2
Outputs:
- orbit: float32 [3, 2, 16, 128, 512], P(None, 'tm', None, 'wall', 'span')
- residual: float32 [3, 2, 16, 128, 512], P(None, 'tm', None, 'wall', 'span')
The draws below stay inside these ranges and needn't reach their ends.
All inputs are finite; a program needn't handle non-finite values.
Results may differ from the reference program's by a relative error of at most 0.0001.
Values sent between devices are 32-bit elements; how exact they have to be, the bound alone decides.
No kernel may reach another device: no remote copies, remote signals or barrier semaphores. Data moves between devices by JAX's collectives and lax.ppermute only.
A program may use at most 64 MiB of HBM per device.

```python
import math
import jax
import jax.numpy as jnp

LENGTHWISE_SLABS = 16
ITERS = 2
TIME_LEVELS = 2
NORMAL_LAYERS = 128
CROSSWISE_POINTS = 512


def steps_of(stream_key, dims, cuts, smallest, largest):
    def one(position, parts):
        heights = jax.random.uniform(jax.random.fold_in(jax.random.fold_in(stream_key, 6), position), (parts,), jnp.float32, smallest / len(cuts), largest / len(cuts))
        return jnp.repeat(jnp.exp(heights), dims[position] // parts).reshape((-1,) + (1,) * (len(dims) - position - 1))

    factor_of = one(*cuts[0])
    for cut in cuts[1:]:
        factor_of = factor_of * one(*cut)
    return factor_of


def noise(key, shape, deviation, reach, cuts=(), kind=jnp.bfloat16):
    entries = deviation * jax.random.normal(key, shape, jnp.float32)
    if cuts:
        entries = entries * steps_of(key, shape, cuts, -0.22, 0.18)
    return jnp.clip(entries, -reach, reach).astype(kind)


def setup_inputs(seed: int = 0) -> dict:
    splits = jax.random.split(jax.random.key(seed), 4)
    return {
        "starting_speed_vector": noise(splits[0], (3, TIME_LEVELS, LENGTHWISE_SLABS, NORMAL_LAYERS, CROSSWISE_POINTS), 1.0, 6.0, ((1, 2), (3, 4), (4, 4)), jnp.float32),
        "driving_source": noise(splits[1], (3, TIME_LEVELS, LENGTHWISE_SLABS, NORMAL_LAYERS, CROSSWISE_POINTS), 0.5, 3.0, ((1, 2), (3, 4), (4, 4)), jnp.float32),
        "viscosity": jnp.clip(jnp.exp(math.log(0.2) - 2.3025851 * jax.random.uniform(splits[2], (NORMAL_LAYERS,), jnp.float32) ** steps_of(splits[2], (NORMAL_LAYERS,), ((0, 4),), -0.2, 0.2)), 0.02, 0.2),
    }


step_rate = 0.05


def forward_cell(values, axis):
    if axis == 3:
        zeros_row = jnp.zeros_like(values[:, :, :, :1])
        return jnp.concatenate((values[:, :, :, 1:], zeros_row), 3)
    return jnp.roll(values, -1, axis)


def backward_cell(values, axis):
    if axis == 3:
        zeros_row = jnp.zeros_like(values[:, :, :, :1])
        return jnp.concatenate((zeros_row, values[:, :, :, :-1]), 3)
    return jnp.roll(values, 1, axis)


def central(values, axis):
    return 0.5 * (forward_cell(values, axis) - backward_cell(values, axis))


def laplacian(values):
    total = forward_cell(values, 2) + backward_cell(values, 2) - 2.0 * values
    total = total + (forward_cell(values, 3) + backward_cell(values, 3) - 2.0 * values)
    return total + (forward_cell(values, 4) + backward_cell(values, 4) - 2.0 * values)


def reflect(values):
    midperiod_translation = TIME_LEVELS // 2
    turned = jnp.roll(values, -midperiod_translation, 1)[:, :, :, ::-1, :]
    sign_row = jnp.array([1.0, -1.0, 1.0], dtype=jnp.float32).reshape(3, 1, 1, 1, 1)
    return turned * sign_row


def reference(starting_speed_vector, driving_source, viscosity):
    viscous = viscosity[None, None, None, :, None]
    present_state = starting_speed_vector
    residual = starting_speed_vector
    for iteration in range(ITERS):
        slopes = [central(present_state, 2 + axis_id) for axis_id in range(3)]
        advect = present_state[0:1] * slopes[0] + present_state[1:2] * slopes[1] + present_state[2:3] * slopes[2]
        residual = (0.5 * (jnp.roll(present_state, -1, 1) - jnp.roll(present_state, 1, 1)) + advect
                    - viscous * laplacian(present_state) + 0.5 * (present_state - reflect(present_state)) - driving_source)
        transport = jnp.stack([jnp.sum(residual * slopes[component], axis=0) for component in range(3)])
        second = (central(present_state[0:1] * residual, 2) + central(present_state[1:2] * residual, 3)
                  + central(present_state[2:3] * residual, 4))
        descent = (-0.5 * (jnp.roll(residual, -1, 1) - jnp.roll(residual, 1, 1)) + transport - second
                   - laplacian(viscous * residual) + 0.5 * (residual - reflect(residual)))
        present_state = present_state - step_rate * descent
    return present_state, residual
```

```python
import functools

import jax
import jax.numpy as jnp
from jax import lax
from jax.experimental import pallas as pl
from jax.experimental.pallas import tpu as pltpu
from jax.sharding import PartitionSpec as P

ITERS = 2


step_rate = 0.05
LANES = 128
SUBLANES = 8
SIGNS = (1.0, -1.0, 1.0)


def instant_weights(instants):
    weights = {}
    for offset, weight in ((1, 0.5), (-1, -0.5)):
        weights[offset % instants] = weights.get(offset % instants, 0.0) + weight
    return {offset: weight for offset, weight in weights.items() if weight != 0.0}


def with_halo(cells, sides, width, closed):
    for axis, dim in sides:
        count = lax.axis_size(axis)
        ends = count if closed else count - 1
        head = lax.slice_in_dim(cells, 0, width, axis=dim)
        tail = lax.slice_in_dim(cells, cells.shape[dim] - width, cells.shape[dim], axis=dim)
        cells = jnp.concatenate(
            [
                lax.ppermute(tail, axis, [(i, (i + 1) % count) for i in range(ends)]),
                cells,
                lax.ppermute(head, axis, [((i + 1) % count, i) for i in range(ends)]),
            ],
            axis=dim,
        )
    return cells


def time_slope(values):
    instants = values.shape[1] * lax.axis_size("tm")
    if not instant_weights(instants):
        return jnp.zeros_like(values)
    padded_state = with_halo(values, (("tm", 1),), 1, True)
    return 0.5 * (padded_state[:, 2:] - padded_state[:, :-2])


def wall_pair(values):
    padded_state = with_halo(values, (("wall", 3),), 1, False)
    return (padded_state[:, :, :, 2:], padded_state[:, :, :, :-2])


def span_pair(values):
    padded_state = with_halo(values, (("span", 4),), 1, True)
    return (padded_state[:, :, :, :, 2:], padded_state[:, :, :, :, :-2])


def along_flow(values):
    return (jnp.roll(values, -1, 2), jnp.roll(values, 1, 2))


def partner_pairs():
    times, walls = lax.axis_size("tm"), lax.axis_size("wall")
    return [
        (time * walls + wall, ((time + times // 2) % times) * walls + walls - 1 - wall)
        for time in range(times)
        for wall in range(walls)
    ]


def reflect(values):
    sign_row = jnp.array(SIGNS, jnp.float32).reshape(3, 1, 1, 1, 1)
    partner = lax.ppermute(values, ("tm", "wall"), partner_pairs())
    return partner[:, :, :, ::-1, :] * sign_row


def residual_of(present_state, mirrored, driving_source, viscous):
    neighbours = (along_flow(present_state), wall_pair(present_state), span_pair(present_state))
    slopes = [0.5 * (ahead - behind) for ahead, behind in neighbours]
    advect = (
        present_state[0:1] * slopes[0]
        + present_state[1:2] * slopes[1]
        + present_state[2:3] * slopes[2]
    )
    laplace = neighbours[0][0] + neighbours[0][1] - 2.0 * present_state
    laplace = laplace + (neighbours[1][0] + neighbours[1][1] - 2.0 * present_state)
    laplace = laplace + (neighbours[2][0] + neighbours[2][1] - 2.0 * present_state)
    residual_now = (
        time_slope(present_state)
        + advect
        - viscous * laplace
        + 0.5 * (present_state - mirrored)
        - driving_source
    )
    return (residual_now, neighbours, slopes)


def descent_part(neighbours, slopes, residual_now, viscous):
    scaled = viscous * residual_now
    wall_ahead, wall_behind = wall_pair(jnp.concatenate((residual_now, scaled), 0))
    flow_ahead, flow_behind = along_flow(residual_now)
    span_ahead, span_behind = span_pair(residual_now)
    residual_pairs = (
        (flow_ahead, flow_behind),
        (wall_ahead[:3], wall_behind[:3]),
        (span_ahead, span_behind),
    )
    transport = jnp.stack(
        [jnp.sum(residual_now * slopes[component], axis=0) for component in range(3)]
    )
    second = None
    for axis_id in range(3):
        ahead_u = neighbours[axis_id][0][axis_id : axis_id + 1]
        behind_u = neighbours[axis_id][1][axis_id : axis_id + 1]
        term = 0.5 * (ahead_u * residual_pairs[axis_id][0] - behind_u * residual_pairs[axis_id][1])
        second = term if second is None else second + term
    diffused = viscous * flow_ahead + viscous * flow_behind - 2.0 * scaled
    diffused = diffused + (wall_ahead[3:] + wall_behind[3:] - 2.0 * scaled)
    diffused = diffused + (viscous * span_ahead + viscous * span_behind - 2.0 * scaled)
    return -time_slope(residual_now) + transport - second - diffused


def staged(starting_speed_vector, driving_source, viscosity):
    viscous = viscosity[None, None, None, :, None]
    present_state = starting_speed_vector
    residual_now = starting_speed_vector
    for iteration in range(ITERS):
        mirrored = reflect(present_state)
        residual_now, neighbours, slopes = residual_of(
            present_state, mirrored, driving_source, viscous
        )
        local_part = descent_part(neighbours, slopes, residual_now, viscous)
        mirror_residual = reflect(residual_now)
        present_state = present_state - step_rate * (
            local_part + 0.5 * (residual_now - mirror_residual)
        )
    return (present_state, residual_now)


def to_tiles(rows_ref, first, planes, tile, depth):
    block = rows_ref[pl.ds(first, planes), pl.ds(tile, SUBLANES, stride=depth), :]
    return block.reshape(planes * SUBLANES, block.shape[-1]).T


def extend_rows(target, source, before, after, offset, count, halo):
    rows = source.shape[1]

    def place(plane, carry):
        target[plane, 0:halo] = before[offset + plane]
        target[plane, halo : halo + rows] = source[plane]
        target[plane, halo + rows : rows + 2 * halo] = after[offset + plane]
        return carry

    lax.fori_loop(0, count, place, 0)


def prepare(planes, halo, speed, force, thickness, before, after, speed_tiles, force_tiles, thick_tiles, first, last, rows):
    count = speed.shape[0]
    cells = speed.shape[-1]
    depth = rows.shape[1] // SUBLANES
    for part, (source, target) in enumerate(((speed, speed_tiles), (force, force_tiles))):
        extend_rows(rows, source, before, after, part * count, count, halo)
        for component in range(3):
            for tile in range(depth):
                place = component * depth + tile
                block = to_tiles(rows, component * planes, planes, tile, depth)
                target[place] = block
                first[part * 3 * depth + place] = block[:halo]
                last[part * 3 * depth + place] = block[cells - halo :]
    extend_rows(rows, thickness, before, after, 2 * count, 1, halo)
    for tile in range(depth):
        block = rows[0, pl.ds(tile, SUBLANES, stride=depth), :]
        block = jnp.concatenate([block] * planes, axis=0).T
        thick_tiles[tile] = block[:SUBLANES]


def turn(block):
    lanes = lax.broadcasted_iota(jnp.int32, block.shape, 1)
    return jnp.take_along_axis(block, lanes ^ (SUBLANES - 1), axis=1)


def wrap(field, cells):
    ring = field.shape[1] - 2 * SUBLANES
    field[:, SUBLANES - 1 : SUBLANES] = field[:, SUBLANES + ring - 1 : SUBLANES + ring]
    field[:, SUBLANES + ring : SUBLANES + ring + 1] = field[:, SUBLANES : SUBLANES + 1]


def row_ahead(tiles, tile):
    return tiles[tile + 1] if tile + 1 < len(tiles) else pltpu.roll(tiles[0], LANES - 1, 1)


def row_behind(tiles, tile):
    return tiles[tile - 1] if tile > 0 else pltpu.roll(tiles[-1], 1, 1)


def plane_ahead(tile):
    return pltpu.roll(tile, LANES - SUBLANES, 1)


def plane_behind(tile):
    return pltpu.roll(tile, SUBLANES, 1)


def load(field, component, depth, start):
    return [field[component * depth + tile, pl.ds(start, SUBLANES), :] for tile in range(depth)]


def residual_stage(speed, mirrored, force, thick, inside, residual, slopes, depth, steps):
    def step(index, carry):
        start = pl.multiple_of(SUBLANES + index * SUBLANES, SUBLANES)
        tiles = [load(speed, component, depth, start) for component in range(3)]
        for tile in range(depth):
            thin = thick[tile]
            half = [0.5 * tiles[component][tile] for component in range(3)]
            for component in range(3):
                place = component * depth + tile
                here = tiles[component][tile]
                pairs = (
                    (plane_ahead(here), plane_behind(here)),
                    (row_ahead(tiles[component], tile), row_behind(tiles[component], tile)),
                    (
                        speed[place, pl.ds(start + 1, SUBLANES), :],
                        speed[place, pl.ds(start - 1, SUBLANES), :],
                    ),
                )
                around = None
                total = None
                for axis_id, (ahead, behind) in enumerate(pairs):
                    slope = ahead - behind
                    if slopes is not None:
                        slopes[axis_id * 3 * depth + place, pl.ds(start, SUBLANES), :] = slope
                    both = ahead + behind
                    around = both if around is None else around + both
                    term = half[axis_id] * slope
                    total = term if total is None else total + term
                laplace = around - 6.0 * here
                other = mirrored[place, pl.ds(start, SUBLANES), :]
                total = total - thin * laplace + 0.5 * (here - other)
                total = total - force[place, pl.ds(start, SUBLANES), :]
                residual[place, pl.ds(start, SUBLANES), :] = total * inside[tile]
        return carry

    lax.fori_loop(0, steps, step, 0)


def descent_stage(speed, residual, mirrored, thick, inside, slopes, following, depth, steps):
    def step(index, carry):
        start = pl.multiple_of(SUBLANES + index * SUBLANES, SUBLANES)
        speeds = [load(speed, component, depth, start) for component in range(3)]
        tiles = [load(residual, component, depth, start) for component in range(3)]
        rises = []
        falls = []
        for tile in range(depth):
            half = 0.5 * speeds[1][tile]
            rises.append(half + thick[tile])
            falls.append(half - thick[tile])
        upper = [[rises[tile] * tiles[c][tile] for tile in range(depth)] for c in range(3)]
        lower = [[falls[tile] * tiles[c][tile] for tile in range(depth)] for c in range(3)]
        for tile in range(depth):
            thin = thick[tile]
            flow = 0.5 * speeds[0][tile]
            flow_rise, flow_fall = flow + thin, flow - thin
            span_rise = 0.5 * speed[2 * depth + tile, pl.ds(start + 1, SUBLANES), :] + thin
            span_fall = 0.5 * speed[2 * depth + tile, pl.ds(start - 1, SUBLANES), :] - thin
            half = [0.5 * tiles[component][tile] for component in range(3)]
            middle = 6.0 * thin
            rate = step_rate * inside[tile]
            for component in range(3):
                place = component * depth + tile
                here = tiles[component][tile]
                total = None
                for inner in range(3):
                    slope = slopes[
                        (component * 3 + inner) * depth + tile, pl.ds(start, SUBLANES), :
                    ]
                    term = half[inner] * slope
                    total = term if total is None else total + term
                total = total - plane_ahead(flow_rise * here) + plane_behind(flow_fall * here)
                total = total - row_ahead(upper[component], tile) + row_behind(lower[component], tile)
                total = total - span_rise * residual[place, pl.ds(start + 1, SUBLANES), :]
                total = total + span_fall * residual[place, pl.ds(start - 1, SUBLANES), :]
                total = total + middle * here
                other = mirrored[place, pl.ds(start, SUBLANES), :]
                total = total + 0.5 * (here - other)
                following[place, pl.ds(start, SUBLANES), :] = speeds[component][tile] - rate * total
        return carry

    lax.fori_loop(0, steps, step, 0)


def iterate(planes, halo, wall, speed_tiles, force_tiles, thick_tiles, ahead_cells, behind_cells,
            partner_speed, partner_force, partner_thick, partner_before, partner_after, partner_ahead, partner_behind,
            speed_out, residual_out,
            rows, own, own_force, own_residual, own_slopes, own_next,
            far, far_force, far_residual, far_slopes, far_next, own_thick, far_thick, inside):
    count, width, cells = partner_speed.shape
    depth = rows.shape[1] // SUBLANES
    blocks = 3 * depth
    ring = own.shape[1] - 2 * SUBLANES
    body = pl.ds(SUBLANES, cells)
    ahead = pl.ds(SUBLANES + cells, halo)
    behind = pl.ds(SUBLANES + cells + halo, halo)

    for part, (field, source) in enumerate(((own, speed_tiles), (own_force, force_tiles))):
        field[:, body] = source[...]
        field[:, ahead] = ahead_cells[pl.ds(part * blocks, blocks)]
        field[:, behind] = behind_cells[pl.ds(part * blocks, blocks)]
        wrap(field, cells)
    for part, (field, source) in enumerate(((far, partner_speed), (far_force, partner_force))):
        extend_rows(rows, source, partner_before, partner_after, part * count, count, halo)
        for component in range(3):
            for tile in range(depth):
                place = component * depth + depth - 1 - tile
                block = to_tiles(rows, component * planes, planes, tile, depth)
                field[place, body] = SIGNS[component] * turn(block)
                got = part * blocks + component * depth + tile
                field[place, ahead] = SIGNS[component] * turn(partner_ahead[got])
                field[place, behind] = SIGNS[component] * turn(partner_behind[got])
        wrap(field, cells)
    lane = lax.broadcasted_iota(jnp.int32, (SUBLANES, LANES), 1) % SUBLANES
    for tile in range(depth):
        own_thick[tile] = thick_tiles[tile]
        far_thick[tile] = turn(partner_thick[depth - 1 - tile])
        row = wall[0] * width - halo + tile + depth * lane
        inside[tile] = jnp.where((row >= 0) & (row < wall[1] * width), 1.0, 0.0).astype(jnp.float32)

    steps = ring // SUBLANES
    for iteration in range(ITERS):
        final = iteration + 1 == ITERS
        residual_stage(own, far, own_force, own_thick, inside, own_residual, own_slopes, depth, steps)
        wrap(own_residual, cells)
        residual_stage(far, own, far_force, far_thick, inside, far_residual, None if final else far_slopes, depth, steps)
        descent_stage(own, own_residual, far_residual, own_thick, inside, own_slopes, own_next, depth,
                      cells // SUBLANES if final else steps)
        if not final:
            wrap(far_residual, cells)
            wrap(own_next, cells)
            descent_stage(far, far_residual, own_residual, far_thick, inside, far_slopes, far_next, depth, steps)
            wrap(far_next, cells)
            own, own_next = own_next, own
            far, far_next = far_next, far

    for field, target in ((own_next, speed_out), (own_residual, residual_out)):
        for component in range(3):
            for tile in range(depth):
                block = field[component * depth + tile, body].T
                block = block.reshape(planes, SUBLANES, cells)
                rows[pl.ds(component * planes, planes), pl.ds(tile, SUBLANES, stride=depth), :] = block
        target[...] = rows[:, halo : halo + width]


def carried(starting_speed_vector, driving_source, viscosity):
    shape = starting_speed_vector.shape
    _, _, planes, width, cells = shape
    halo = 2 * ITERS
    depth = (width + 2 * halo) // SUBLANES
    blocks = 3 * depth
    count = 3 * planes
    whole = pl.BlockSpec(memory_space=pltpu.VMEM)
    arrays = lambda *sizes: jax.ShapeDtypeStruct(sizes, jnp.float32)
    speed = starting_speed_vector.reshape(count, width, cells)
    force = driving_source.reshape(count, width, cells)
    thickness = jnp.broadcast_to(viscosity[None, :, None], (1, width, cells))

    to_partner = functools.partial(lax.ppermute, axis_name=("tm", "wall"), perm=partner_pairs())
    walls, spans = lax.axis_size("wall"), lax.axis_size("span")
    upward = [(i, i + 1) for i in range(walls - 1)]
    downward = [(i + 1, i) for i in range(walls - 1)]
    onward = [(i, (i + 1) % spans) for i in range(spans)]
    backward = [((i + 1) % spans, i) for i in range(spans)]

    partner_speed = to_partner(speed)
    partner_force = to_partner(force)
    stack = lambda part: jnp.concatenate([part(speed), part(force), part(thickness)])
    before = lax.ppermute(stack(lambda a: a[:, width - halo :]), "wall", upward)
    after = lax.ppermute(stack(lambda a: a[:, :halo]), "wall", downward)
    speed_tiles, force_tiles, thick_tiles, first, last = pl.pallas_call(
        functools.partial(prepare, planes, halo),
        out_shape=(
            arrays(blocks, cells, LANES),
            arrays(blocks, cells, LANES),
            arrays(depth, SUBLANES, LANES),
            arrays(2 * blocks, halo, LANES),
            arrays(2 * blocks, halo, LANES),
        ),
        in_specs=[whole] * 5,
        out_specs=[whole] * 5,
        scratch_shapes=[pltpu.VMEM((count, width + 2 * halo, cells), jnp.float32)],
        compiler_params=pltpu.CompilerParams(vmem_limit_bytes=32 * 2**20),
        name="prepare",
    )(speed, force, thickness, before, after)
    behind_cells = lax.ppermute(last, "span", onward)
    ahead_cells = lax.ppermute(first, "span", backward)
    partner_before = to_partner(before)
    partner_after = to_partner(after)
    partner_thick = to_partner(thick_tiles)
    partner_ahead = to_partner(ahead_cells)
    partner_behind = to_partner(behind_cells)

    wall = jnp.stack([lax.axis_index("wall"), jnp.int32(walls)])
    field = pltpu.VMEM((blocks, cells + 2 * halo + 2 * SUBLANES, LANES), jnp.float32)
    slope = pltpu.VMEM((3 * blocks, cells + 2 * halo + 2 * SUBLANES, LANES), jnp.float32)
    small = pltpu.VMEM((depth, SUBLANES, LANES), jnp.float32)
    speed_out, residual_out = pl.pallas_call(
        functools.partial(iterate, planes, halo),
        out_shape=(arrays(count, width, cells), arrays(count, width, cells)),
        in_specs=[pl.BlockSpec(memory_space=pltpu.SMEM)] + [whole] * 12,
        out_specs=[whole] * 2,
        scratch_shapes=[pltpu.VMEM((count, width + 2 * halo, cells), jnp.float32)]
        + [field, field, field, slope, field] * 2
        + [small] * 3,
        compiler_params=pltpu.CompilerParams(vmem_limit_bytes=48 * 2**20),
        name="iterate",
    )(wall, speed_tiles, force_tiles, thick_tiles, ahead_cells, behind_cells,
      partner_speed, partner_force, partner_thick, partner_before, partner_after, partner_ahead, partner_behind)
    return speed_out.reshape(shape), residual_out.reshape(shape)


def local(starting_speed_vector, driving_source, viscosity):
    _, instants, planes, width, cells = starting_speed_vector.shape
    times = lax.axis_size("tm") * instants
    halo = 2 * ITERS
    one_instant = instants == 1 and not instant_weights(times)
    tiled = planes * SUBLANES == LANES and cells % LANES == 0 and (width + 2 * halo) % SUBLANES == 0
    if one_instant and tiled and (2 * halo) % SUBLANES == 0 and halo <= width:
        return carried(starting_speed_vector, driving_source, viscosity)
    return staged(starting_speed_vector, driving_source, viscosity)


def solution(mesh):
    placed = (P(None, "tm", None, "wall", "span"), P(None, "tm", None, "wall", "span"), P("wall"))
    return jax.shard_map(
        local,
        mesh=mesh,
        in_specs=placed,
        out_specs=(P(None, "tm", None, "wall", "span"), P(None, "tm", None, "wall", "span")),
        check_vma=False,
    )
```

```python
import functools

import jax
import jax.numpy as jnp
from jax import lax
from jax.experimental import pallas as pl
from jax.experimental.pallas import tpu as pltpu
from jax.sharding import PartitionSpec as P

ITERS = 2


step_rate = 0.05
LANES = 128
SUBLANES = 8
SIGNS = (1.0, -1.0, 1.0)


def instant_weights(instants):
    weights = {}
    for offset, weight in ((1, 0.5), (-1, -0.5)):
        weights[offset % instants] = weights.get(offset % instants, 0.0) + weight
    return {offset: weight for offset, weight in weights.items() if weight != 0.0}


def with_halo(cells, sides, width, closed):
    for axis, dim in sides:
        count = lax.axis_size(axis)
        ends = count if closed else count - 1
        head = lax.slice_in_dim(cells, 0, width, axis=dim)
        tail = lax.slice_in_dim(cells, cells.shape[dim] - width, cells.shape[dim], axis=dim)
        cells = jnp.concatenate(
            [
                lax.ppermute(tail, axis, [(i, (i + 1) % count) for i in range(ends)]),
                cells,
                lax.ppermute(head, axis, [((i + 1) % count, i) for i in range(ends)]),
            ],
            axis=dim,
        )
    return cells


def time_slope(values):
    instants = values.shape[1] * lax.axis_size("tm")
    if not instant_weights(instants):
        return jnp.zeros_like(values)
    padded_state = with_halo(values, (("tm", 1),), 1, True)
    return 0.5 * (padded_state[:, 2:] - padded_state[:, :-2])


def wall_pair(values):
    padded_state = with_halo(values, (("wall", 3),), 1, False)
    return (padded_state[:, :, :, 2:], padded_state[:, :, :, :-2])


def span_pair(values):
    padded_state = with_halo(values, (("span", 4),), 1, True)
    return (padded_state[:, :, :, :, 2:], padded_state[:, :, :, :, :-2])


def along_flow(values):
    return (jnp.roll(values, -1, 2), jnp.roll(values, 1, 2))


def partner_pairs():
    times, walls = lax.axis_size("tm"), lax.axis_size("wall")
    return [
        (time * walls + wall, ((time + times // 2) % times) * walls + walls - 1 - wall)
        for time in range(times)
        for wall in range(walls)
    ]


def reflect(values):
    sign_row = jnp.array(SIGNS, jnp.float32).reshape(3, 1, 1, 1, 1)
    partner = lax.ppermute(values, ("tm", "wall"), partner_pairs())
    return partner[:, :, :, ::-1, :] * sign_row


def residual_of(present_state, mirrored, driving_source, viscous):
    neighbours = (along_flow(present_state), wall_pair(present_state), span_pair(present_state))
    slopes = [0.5 * (ahead - behind) for ahead, behind in neighbours]
    advect = (
        present_state[0:1] * slopes[0]
        + present_state[1:2] * slopes[1]
        + present_state[2:3] * slopes[2]
    )
    laplace = neighbours[0][0] + neighbours[0][1] - 2.0 * present_state
    laplace = laplace + (neighbours[1][0] + neighbours[1][1] - 2.0 * present_state)
    laplace = laplace + (neighbours[2][0] + neighbours[2][1] - 2.0 * present_state)
    residual_now = (
        time_slope(present_state)
        + advect
        - viscous * laplace
        + 0.5 * (present_state - mirrored)
        - driving_source
    )
    return (residual_now, neighbours, slopes)


def descent_part(neighbours, slopes, residual_now, viscous):
    scaled = viscous * residual_now
    wall_ahead, wall_behind = wall_pair(jnp.concatenate((residual_now, scaled), 0))
    flow_ahead, flow_behind = along_flow(residual_now)
    span_ahead, span_behind = span_pair(residual_now)
    residual_pairs = (
        (flow_ahead, flow_behind),
        (wall_ahead[:3], wall_behind[:3]),
        (span_ahead, span_behind),
    )
    transport = jnp.stack(
        [jnp.sum(residual_now * slopes[component], axis=0) for component in range(3)]
    )
    second = None
    for axis_id in range(3):
        ahead_u = neighbours[axis_id][0][axis_id : axis_id + 1]
        behind_u = neighbours[axis_id][1][axis_id : axis_id + 1]
        term = 0.5 * (ahead_u * residual_pairs[axis_id][0] - behind_u * residual_pairs[axis_id][1])
        second = term if second is None else second + term
    diffused = viscous * flow_ahead + viscous * flow_behind - 2.0 * scaled
    diffused = diffused + (wall_ahead[3:] + wall_behind[3:] - 2.0 * scaled)
    diffused = diffused + (viscous * span_ahead + viscous * span_behind - 2.0 * scaled)
    return -time_slope(residual_now) + transport - second - diffused


def staged(starting_speed_vector, driving_source, viscosity):
    viscous = viscosity[None, None, None, :, None]
    present_state = starting_speed_vector
    residual_now = starting_speed_vector
    for iteration in range(ITERS):
        mirrored = reflect(present_state)
        residual_now, neighbours, slopes = residual_of(
            present_state, mirrored, driving_source, viscous
        )
        local_part = descent_part(neighbours, slopes, residual_now, viscous)
        mirror_residual = reflect(residual_now)
        present_state = present_state - step_rate * (
            local_part + 0.5 * (residual_now - mirror_residual)
        )
    return (present_state, residual_now)


GROUP = 17


def sweep(steps, step):
    rounds = steps // GROUP

    def several(index, carry):
        for inner in range(GROUP):
            step(pl.multiple_of((index * GROUP + inner + 1) * SUBLANES, SUBLANES))
        return carry

    if rounds > 1:
        lax.fori_loop(0, rounds, several, 0)
    done = rounds * GROUP if rounds > 1 else 0
    for index in range(done, steps):
        step((index + 1) * SUBLANES)


def edges(halo, speed_first, speed_last, force_first, force_last, thickness, own_first, own_last):
    count = speed_first.shape[0] // SUBLANES
    fields = ((speed_first, speed_last, halo), (force_first, force_last, halo - 1))
    at = 0
    for first, last, held in fields:
        for row in range(held):
            for plane in range(0, count, SUBLANES):
                start = plane * SUBLANES
                own_first[at : at + SUBLANES] = first[pl.ds(start + row, SUBLANES, stride=SUBLANES), :]
                own_last[at : at + SUBLANES] = last[pl.ds(start + SUBLANES - 1 - row, SUBLANES, stride=SUBLANES), :]
                at += SUBLANES
    spread = jnp.broadcast_to(thickness[...], (SUBLANES, LANES))
    own_first[at : at + SUBLANES] = spread
    own_last[at : at + SUBLANES] = spread


def planes_of(*parts):
    return [part.at[plane] for part in parts for plane in range(part.shape[0])]


def extend_rows(rows, source, before, after, offset, held, halo):
    count, width = len(source), source[0].shape[0]
    extended = width + 2 * halo
    for plane in range(count):
        rows[pl.ds(plane * extended + halo, width), :] = source[plane][...]
    for row in range(halo):
        for plane in range(0, count, SUBLANES):
            at = offset + row * count + plane
            for edge, place in ((before, halo - 1 - row), (after, halo + width + row)):
                block = edge[pl.ds(at, SUBLANES), :] if row < held else jnp.zeros((SUBLANES, LANES), jnp.float32)
                rows[pl.ds(plane * extended + place, SUBLANES, stride=extended), :] = block


def to_tiles(rows, component, planes, tile, depth):
    extended = depth * SUBLANES
    blocks = [
        rows[pl.ds((component * planes + plane) * extended + tile, SUBLANES, stride=depth), :]
        for plane in range(planes)
    ]
    return jnp.concatenate(blocks, axis=0).T


def prepare(planes, halo, speed, force, before, after, speed_tiles, force_tiles, first, last, rows):
    count, width, cells = speed.shape
    depth = (width + 2 * halo) // SUBLANES
    blocks = 3 * depth
    fields = ((speed, speed_tiles, halo, 0), (force, force_tiles, halo - 1, halo * count))
    for part, (source, target, held, offset) in enumerate(fields):
        extend_rows(rows, planes_of(source), before, after, offset, held, halo)
        for component in range(3):
            for tile in range(depth):
                place = component * depth + tile
                block = to_tiles(rows, component, planes, tile, depth)
                target[place] = block
                first[part * blocks + place] = block[:halo]
                last[part * blocks + place] = block[cells - halo :]


def far_sizes(count, blocks, halo):
    rows = (2 * halo - 3) * count
    cells = -(-(2 * halo - 3) * blocks // SUBLANES) * SUBLANES
    return (0, rows, 2 * rows, 2 * rows + cells, 2 * rows + 2 * cells, 2 * rows + 2 * cells + SUBLANES)


def bundle(count, width, halo, before, after, ahead_cells, behind_cells, thickness, pack):
    blocks = ahead_cells.shape[0] // 2
    starts = far_sizes(count, blocks, halo)
    speed_rows = (halo - 1) * count
    force_rows = (halo - 2) * count
    for source, start in ((before, starts[0]), (after, starts[1])):
        pack[start : start + speed_rows] = source[:speed_rows]
        pack[start + speed_rows : start + speed_rows + force_rows] = source[halo * count : halo * count + force_rows]
    for source, start, last in ((ahead_cells, starts[2], False), (behind_cells, starts[3], True)):
        at = start
        for part, held in ((0, halo - 1), (1, halo - 2)):
            for cell in range(held):
                from_edge = halo - 1 - cell if last else cell
                for place in range(blocks):
                    pack[at : at + 1] = source[part * blocks + place, from_edge : from_edge + 1]
                    at += 1
    held = before.shape[0] - SUBLANES
    lane = lax.broadcasted_iota(jnp.int32, (SUBLANES, LANES), 1)
    spread = jnp.broadcast_to(thickness[...], (SUBLANES, LANES))
    parts = jnp.where(lane < width, before[held : held + SUBLANES], pltpu.roll(spread, width, 1))
    parts = jnp.where(lane < 2 * width, parts, pltpu.roll(after[held : held + SUBLANES], 2 * width, 1))
    pack[starts[4] : starts[5]] = parts


def hold(*refs):
    pass


def turn(block):
    lanes = lax.broadcasted_iota(jnp.int32, block.shape, 1)
    return jnp.take_along_axis(block, lanes ^ (SUBLANES - 1), axis=1)


def wrap(field):
    ring = field.shape[1] - 2 * SUBLANES
    field[:, SUBLANES - 1 : SUBLANES] = field[:, SUBLANES + ring - 1 : SUBLANES + ring]
    field[:, SUBLANES + ring : SUBLANES + ring + 1] = field[:, SUBLANES : SUBLANES + 1]


def turned_tiles(field, source, pack, part, planes, halo, rows):
    count = len(source)
    width, cells = source[0].shape
    depth = (width + 2 * halo) // SUBLANES
    blocks = 3 * depth
    starts = far_sizes(count, blocks, halo)
    held = halo - 1 - part
    extend_rows(rows, source, pack.at[starts[0] : starts[1]], pack.at[starts[1] : starts[2]], part * (halo - 1) * count, held, halo)
    for component in range(3):
        for tile in range(depth):
            place = component * depth + depth - 1 - tile
            block = turn(to_tiles(rows, component, planes, tile, depth))
            field[place, SUBLANES : SUBLANES + cells] = -block if SIGNS[component] < 0 else block
    offset = part * (halo - 1) * blocks
    for start, end, base, way in (
        (starts[2], starts[3], SUBLANES + cells, 1),
        (starts[3], starts[4], SUBLANES + cells + 2 * halo - 1, -1),
    ):
        edge = turn(pack[start:end])
        for cell in range(halo):
            for component in range(3):
                for tile in range(depth):
                    place = component * depth + depth - 1 - tile
                    at = offset + cell * blocks + component * depth + tile
                    line = edge[at : at + 1] if cell < held else jnp.zeros((1, LANES), jnp.float32)
                    field[place, base + way * cell : base + way * cell + 1] = -line if SIGNS[component] < 0 else line
    wrap(field)


def row_ahead(tiles, tile):
    return tiles[tile + 1] if tile + 1 < len(tiles) else pltpu.roll(tiles[0], LANES - 1, 1)


def row_behind(tiles, tile):
    return tiles[tile - 1] if tile > 0 else pltpu.roll(tiles[-1], 1, 1)


def plane_ahead(tile):
    return pltpu.roll(tile, LANES - SUBLANES, 1)


def plane_behind(tile):
    return pltpu.roll(tile, SUBLANES, 1)


def load(field, component, depth, start):
    return [field[component * depth + tile, pl.ds(start, SUBLANES), :] for tile in range(depth)]


def residual_stage(speed, mirrored, force, thick, inside, residual, slopes, steps):
    depth = thick.shape[0]

    def step(start):
        tiles = [load(speed, component, depth, start) for component in range(3)]
        for tile in range(depth):
            thin = thick[tile]
            middle = 6.0 * thin + 0.5
            half = [0.5 * tiles[component][tile] for component in range(3)]
            for component in range(3):
                place = component * depth + tile
                here = tiles[component][tile]
                pairs = (
                    (plane_ahead(here), plane_behind(here)),
                    (row_ahead(tiles[component], tile), row_behind(tiles[component], tile)),
                    (
                        speed[place, pl.ds(start + 1, SUBLANES), :],
                        speed[place, pl.ds(start - 1, SUBLANES), :],
                    ),
                )
                around = None
                total = None
                for axis_id, (ahead, behind) in enumerate(pairs):
                    slope = ahead - behind
                    if slopes is not None:
                        slopes[axis_id * 3 * depth + place, pl.ds(start, SUBLANES), :] = slope
                    both = ahead + behind
                    around = both if around is None else around + both
                    term = half[axis_id] * slope
                    total = term if total is None else total + term
                total = total - thin * around + middle * here
                total = total - 0.5 * mirrored[place, pl.ds(start, SUBLANES), :]
                if force is not None:
                    total = (total - force[place, pl.ds(start, SUBLANES), :]) * inside[tile]
                residual[place, pl.ds(start, SUBLANES), :] = total

    sweep(steps, step)


def descent_stage(speed, residual, mirrored, thick, inside, slopes, following, steps):
    depth = thick.shape[0]

    def step(start):
        speeds = [load(speed, component, depth, start) for component in range(3)]
        tiles = [load(residual, component, depth, start) for component in range(3)]
        rises = []
        falls = []
        for tile in range(depth):
            half = 0.5 * speeds[1][tile]
            rises.append(half + thick[tile])
            falls.append(half - thick[tile])
        upper = [[rises[tile] * tiles[c][tile] for tile in range(depth)] for c in range(3)]
        lower = [[falls[tile] * tiles[c][tile] for tile in range(depth)] for c in range(3)]
        for tile in range(depth):
            thin = thick[tile]
            flow = 0.5 * speeds[0][tile]
            flow_rise, flow_fall = flow + thin, flow - thin
            span_rise = 0.5 * speed[2 * depth + tile, pl.ds(start + 1, SUBLANES), :] + thin
            span_fall = 0.5 * speed[2 * depth + tile, pl.ds(start - 1, SUBLANES), :] - thin
            half = [0.5 * tiles[component][tile] for component in range(3)]
            middle = 6.0 * thin + 0.5
            rate = step_rate * inside[tile]
            for component in range(3):
                place = component * depth + tile
                here = tiles[component][tile]
                total = middle * here
                for inner in range(3):
                    slope = slopes[
                        (component * 3 + inner) * depth + tile, pl.ds(start, SUBLANES), :
                    ]
                    total = total + half[inner] * slope
                total = total - plane_ahead(flow_rise * here) + plane_behind(flow_fall * here)
                total = total - row_ahead(upper[component], tile) + row_behind(lower[component], tile)
                total = total - span_rise * residual[place, pl.ds(start + 1, SUBLANES), :]
                total = total + span_fall * residual[place, pl.ds(start - 1, SUBLANES), :]
                if mirrored is not None:
                    total = total - 0.5 * mirrored[place, pl.ds(start, SUBLANES), :]
                following[place, pl.ds(start, SUBLANES), :] = speeds[component][tile] - rate * total

    sweep(steps, step)


def before_force(planes, halo, wall, thickness, before, after, speed_tiles, force_tiles, ahead_cells, behind_cells,
                 partner_1, pack,
                 own_force, far, own_residual, far_open, own_open, far_slopes, own_thick, far_thick, inside,
                 own, own_slopes, rows):
    count = 3 * planes
    _, width, cells = partner_1.shape
    depth = own_thick.shape[0]
    blocks = 3 * depth
    for part, (field, source) in enumerate(((own, speed_tiles), (own_force, force_tiles))):
        field[:, SUBLANES : SUBLANES + cells] = source[...]
        field[:, SUBLANES + cells : SUBLANES + cells + halo] = ahead_cells[part * blocks : part * blocks + blocks]
        field[:, SUBLANES + cells + halo : SUBLANES + cells + 2 * halo] = behind_cells[part * blocks : part * blocks + blocks]
    wrap(own)
    lane = lax.broadcasted_iota(jnp.int32, (SUBLANES, LANES), 1)
    starts = far_sizes(count, blocks, halo)
    far_spread = pack[starts[4] : starts[5]]
    held = before.shape[0] - SUBLANES
    spread = jnp.broadcast_to(thickness[...], (SUBLANES, LANES))
    own_spread = jnp.where(lane < width, before[held : held + SUBLANES], pltpu.roll(spread, width, 1))
    own_spread = jnp.where(lane < 2 * width, own_spread, pltpu.roll(after[held : held + SUBLANES], 2 * width, 1))
    for tile in range(depth):
        row = tile - halo + depth * (lane % SUBLANES)
        own_thick[tile] = jnp.take_along_axis(own_spread, width + row, axis=1)
        far_thick[tile] = jnp.take_along_axis(far_spread, 2 * width - 1 - row, axis=1)
        row = wall[0] * width + row
        inside[tile] = jnp.where((row >= 0) & (row < wall[1] * width), 1.0, 0.0).astype(jnp.float32)
    turned_tiles(far, planes_of(partner_1), pack, 0, planes, halo, rows)
    steps = (cells + 2 * halo) // SUBLANES
    residual_stage(own, far, own_force, own_thick, inside, own_residual, own_slopes, steps)
    wrap(own_residual)
    residual_stage(far, own, None, far_thick, inside, far_open, far_slopes, steps)
    descent_stage(own, own_residual, None, own_thick, inside, own_slopes, own_open, steps)


def with_force(planes, halo, partner_2, partner_3, pack,
               own_force, far, own_residual, far_open, own_open, far_slopes, own_thick, far_thick, inside,
               speed_out, residual_out,
               rows, far_force, far_residual, next_residual, own, next_own, next_far, own_slopes):
    count = 3 * planes
    _, width, cells = partner_3.shape
    depth = own_thick.shape[0]
    blocks = 3 * depth
    turned_tiles(far_force, planes_of(partner_2, partner_3), pack, 1, planes, halo, rows)
    steps = (cells + 2 * halo) // SUBLANES

    def close(start):
        for place in range(blocks):
            at = pl.ds(start, SUBLANES)
            now = (far_open[place, at, :] - far_force[place, at, :]) * inside[place % depth]
            far_residual[place, at, :] = now
            own[place, at, :] = own_open[place, at, :] + (0.5 * step_rate) * now

    sweep(steps, close)
    wrap(far_residual)
    wrap(own)
    descent_stage(far, far_residual, own_residual, far_thick, inside, far_slopes, next_far, steps)
    wrap(next_far)
    far = next_far
    residual_stage(own, far, own_force, own_thick, inside, next_residual, own_slopes, steps)
    wrap(next_residual)
    residual_stage(far, own, far_force, far_thick, inside, far_residual, None, cells // SUBLANES)
    descent_stage(own, next_residual, far_residual, own_thick, inside, own_slopes, next_own, cells // SUBLANES)

    extended = depth * SUBLANES
    for field, target in ((next_residual, residual_out), (next_own, speed_out)):
        for component in range(3):
            for tile in range(depth):
                block = field[component * depth + tile, SUBLANES : SUBLANES + cells].T
                for plane in range(planes):
                    at = (component * planes + plane) * extended + tile
                    rows[pl.ds(at, SUBLANES, stride=depth), :] = block[plane * SUBLANES : (plane + 1) * SUBLANES]
        for plane in range(count):
            target[plane] = rows[pl.ds(plane * extended + halo, width), :]


def carried(starting_speed_vector, driving_source, viscosity):
    shape = starting_speed_vector.shape
    _, _, planes, width, cells = shape
    halo = 2 * ITERS
    depth = (width + 2 * halo) // SUBLANES
    blocks = 3 * depth
    count = 3 * planes
    whole = pl.BlockSpec(memory_space=pltpu.VMEM)
    arrays = lambda *sizes: jax.ShapeDtypeStruct(sizes, jnp.float32)
    grant = lambda mega: pltpu.CompilerParams(vmem_limit_bytes=mega * 2**20)
    tall = cells + 2 * halo + 2 * SUBLANES
    rows = pltpu.VMEM((count * (width + 2 * halo), cells), jnp.float32)
    field = pltpu.VMEM((blocks, tall, LANES), jnp.float32)
    slope = pltpu.VMEM((3 * blocks, tall, LANES), jnp.float32)
    speed = starting_speed_vector.reshape(count, width, cells)
    force = driving_source.reshape(count, width, cells)

    walls, spans = lax.axis_size("wall"), lax.axis_size("span")
    upward = [(i, i + 1) for i in range(walls - 1)]
    downward = [(i + 1, i) for i in range(walls - 1)]
    onward = [(i, (i + 1) % spans) for i in range(spans)]
    backward = [((i + 1) % spans, i) for i in range(spans)]
    to_partner = functools.partial(lax.ppermute, axis_name=("tm", "wall"), perm=partner_pairs())

    cut = count * 17 // 24
    partner_1 = to_partner(speed)
    sent_2 = force[:cut]
    sent_3 = force[cut:]
    any_place = pl.BlockSpec(memory_space=pl.ANY)
    after_all = lambda held, *others: pl.pallas_call(
        hold,
        out_shape=arrays(*held.shape),
        in_specs=[any_place] * (1 + len(others)),
        out_specs=any_place,
        input_output_aliases={0: 0},
        name="hold",
    )(held, *others)

    thickness = jnp.pad(viscosity, (0, LANES - width)).reshape(1, LANES)
    tops = pl.BlockSpec((count, SUBLANES, cells), lambda i: (0, 0, 0))
    ends = pl.BlockSpec((count, SUBLANES, cells), lambda i: (0, width // SUBLANES - 1, 0))
    lines = (2 * halo - 1) * count + SUBLANES
    flat = lambda ref: ref.reshape(count * SUBLANES, cells)
    own_first, own_last = pl.pallas_call(
        lambda a, b, c, d, *rest: edges(halo, flat(a), flat(b), flat(c), flat(d), *rest),
        out_shape=(arrays(lines, cells),) * 2,
        grid=(1,),
        in_specs=[tops, ends, tops, ends, pl.BlockSpec((1, LANES), lambda i: (0, 0))],
        out_specs=[pl.BlockSpec((lines, cells), lambda i: (0, 0))] * 2,
        compiler_params=grant(8),
        name="edges",
    )(speed, speed, force, force, thickness)
    before = lax.ppermute(own_last, "wall", upward)
    after = lax.ppermute(own_first, "wall", downward)
    partner_2 = to_partner(after_all(sent_2, before, after))
    speed_tiles, force_tiles, first, last = pl.pallas_call(
        functools.partial(prepare, planes, halo),
        out_shape=(arrays(blocks, cells, LANES),) * 2 + (arrays(2 * blocks, halo, LANES),) * 2,
        in_specs=[whole] * 4,
        out_specs=[whole] * 4,
        scratch_shapes=[rows],
        compiler_params=grant(12),
        name="prepare",
    )(speed, force, before, after)
    behind_cells = lax.ppermute(last, "span", onward)
    ahead_cells = lax.ppermute(first, "span", backward)
    pack = pl.pallas_call(
        functools.partial(bundle, count, width, halo),
        out_shape=arrays(far_sizes(count, blocks, halo)[-1], LANES),
        in_specs=[whole] * 5,
        out_specs=whole,
        compiler_params=grant(8),
        name="bundle",
    )(before, after, ahead_cells, behind_cells, thickness)
    far_pack = to_partner(pack)
    partner_3 = to_partner(after_all(sent_3, far_pack))

    wall = jnp.stack([lax.axis_index("wall"), jnp.int32(walls)])
    early = pl.pallas_call(
        functools.partial(before_force, planes, halo),
        out_shape=(arrays(blocks, tall, LANES),) * 5
        + (arrays(3 * blocks, tall, LANES),)
        + (arrays(depth, SUBLANES, LANES),) * 3,
        in_specs=[pl.BlockSpec(memory_space=pltpu.SMEM)] + [whole] * 9,
        out_specs=[whole] * 9,
        scratch_shapes=[field, slope, rows],
        compiler_params=grant(24),
        name="before_force",
    )(wall, thickness, before, after, speed_tiles, force_tiles, ahead_cells, behind_cells,
      partner_1, far_pack)
    speed_out, residual_out = pl.pallas_call(
        functools.partial(with_force, planes, halo),
        out_shape=(arrays(count, width, cells), arrays(count, width, cells)),
        in_specs=[whole] * 12,
        out_specs=[whole] * 2,
        scratch_shapes=[rows] + [field] * 6 + [slope],
        compiler_params=grant(32),
        name="with_force",
    )(partner_2, partner_3, far_pack, *early)
    return speed_out.reshape(shape), residual_out.reshape(shape)


def local(starting_speed_vector, driving_source, viscosity):
    _, instants, planes, width, cells = starting_speed_vector.shape
    times = lax.axis_size("tm") * instants
    halo = 2 * ITERS
    one_instant = ITERS == 2 and instants == 1 and not instant_weights(times)
    tiled = planes * SUBLANES == LANES and cells == LANES and (width + 2 * halo) % SUBLANES == 0
    rows_fit = halo <= width and 3 * width <= LANES and (2 * halo) % SUBLANES == 0
    if one_instant and tiled and rows_fit:
        return carried(starting_speed_vector, driving_source, viscosity)
    return staged(starting_speed_vector, driving_source, viscosity)


def solution(mesh):
    placed = (P(None, "tm", None, "wall", "span"), P(None, "tm", None, "wall", "span"), P("wall"))
    return jax.shard_map(
        local,
        mesh=mesh,
        in_specs=placed,
        out_specs=(P(None, "tm", None, "wall", "span"), P(None, "tm", None, "wall", "span")),
        check_vma=False,
    )
```

```python
import functools

import jax
import jax.numpy as jnp
from jax import lax
from jax.experimental import pallas as pl
from jax.experimental.pallas import tpu as pltpu
from jax.sharding import PartitionSpec as P

ITERS = 2


step_rate = 0.05
LANES = 128
SUBLANES = 8
SIGNS = (1.0, -1.0, 1.0)


def instant_weights(instants):
    weights = {}
    for offset, weight in ((1, 0.5), (-1, -0.5)):
        weights[offset % instants] = weights.get(offset % instants, 0.0) + weight
    return {offset: weight for offset, weight in weights.items() if weight != 0.0}


def with_halo(cells, sides, width, closed):
    for axis, dim in sides:
        count = lax.axis_size(axis)
        ends = count if closed else count - 1
        head = lax.slice_in_dim(cells, 0, width, axis=dim)
        tail = lax.slice_in_dim(cells, cells.shape[dim] - width, cells.shape[dim], axis=dim)
        cells = jnp.concatenate(
            [
                lax.ppermute(tail, axis, [(i, (i + 1) % count) for i in range(ends)]),
                cells,
                lax.ppermute(head, axis, [((i + 1) % count, i) for i in range(ends)]),
            ],
            axis=dim,
        )
    return cells


def time_slope(values):
    instants = values.shape[1] * lax.axis_size("tm")
    if not instant_weights(instants):
        return jnp.zeros_like(values)
    padded_state = with_halo(values, (("tm", 1),), 1, True)
    return 0.5 * (padded_state[:, 2:] - padded_state[:, :-2])


def wall_pair(values):
    padded_state = with_halo(values, (("wall", 3),), 1, False)
    return (padded_state[:, :, :, 2:], padded_state[:, :, :, :-2])


def span_pair(values):
    padded_state = with_halo(values, (("span", 4),), 1, True)
    return (padded_state[:, :, :, :, 2:], padded_state[:, :, :, :, :-2])


def along_flow(values):
    return (jnp.roll(values, -1, 2), jnp.roll(values, 1, 2))


def partner_pairs():
    times, walls = lax.axis_size("tm"), lax.axis_size("wall")
    return [
        (time * walls + wall, ((time + times // 2) % times) * walls + walls - 1 - wall)
        for time in range(times)
        for wall in range(walls)
    ]


def reflect(values):
    sign_row = jnp.array(SIGNS, jnp.float32).reshape(3, 1, 1, 1, 1)
    partner = lax.ppermute(values, ("tm", "wall"), partner_pairs())
    return partner[:, :, :, ::-1, :] * sign_row


def residual_of(present_state, mirrored, driving_source, viscous):
    neighbours = (along_flow(present_state), wall_pair(present_state), span_pair(present_state))
    slopes = [0.5 * (ahead - behind) for ahead, behind in neighbours]
    advect = (
        present_state[0:1] * slopes[0]
        + present_state[1:2] * slopes[1]
        + present_state[2:3] * slopes[2]
    )
    laplace = neighbours[0][0] + neighbours[0][1] - 2.0 * present_state
    laplace = laplace + (neighbours[1][0] + neighbours[1][1] - 2.0 * present_state)
    laplace = laplace + (neighbours[2][0] + neighbours[2][1] - 2.0 * present_state)
    residual_now = (
        time_slope(present_state)
        + advect
        - viscous * laplace
        + 0.5 * (present_state - mirrored)
        - driving_source
    )
    return (residual_now, neighbours, slopes)


def descent_part(neighbours, slopes, residual_now, viscous):
    scaled = viscous * residual_now
    wall_ahead, wall_behind = wall_pair(jnp.concatenate((residual_now, scaled), 0))
    flow_ahead, flow_behind = along_flow(residual_now)
    span_ahead, span_behind = span_pair(residual_now)
    residual_pairs = (
        (flow_ahead, flow_behind),
        (wall_ahead[:3], wall_behind[:3]),
        (span_ahead, span_behind),
    )
    transport = jnp.stack(
        [jnp.sum(residual_now * slopes[component], axis=0) for component in range(3)]
    )
    second = None
    for axis_id in range(3):
        ahead_u = neighbours[axis_id][0][axis_id : axis_id + 1]
        behind_u = neighbours[axis_id][1][axis_id : axis_id + 1]
        term = 0.5 * (ahead_u * residual_pairs[axis_id][0] - behind_u * residual_pairs[axis_id][1])
        second = term if second is None else second + term
    diffused = viscous * flow_ahead + viscous * flow_behind - 2.0 * scaled
    diffused = diffused + (wall_ahead[3:] + wall_behind[3:] - 2.0 * scaled)
    diffused = diffused + (viscous * span_ahead + viscous * span_behind - 2.0 * scaled)
    return -time_slope(residual_now) + transport - second - diffused


def staged(starting_speed_vector, driving_source, viscosity):
    viscous = viscosity[None, None, None, :, None]
    present_state = starting_speed_vector
    residual_now = starting_speed_vector
    for iteration in range(ITERS):
        mirrored = reflect(present_state)
        residual_now, neighbours, slopes = residual_of(
            present_state, mirrored, driving_source, viscous
        )
        local_part = descent_part(neighbours, slopes, residual_now, viscous)
        mirror_residual = reflect(residual_now)
        present_state = present_state - step_rate * (
            local_part + 0.5 * (residual_now - mirror_residual)
        )
    return (present_state, residual_now)


GROUP = 17


def sweep(steps, step):
    rounds = steps // GROUP

    def several(index, carry):
        for inner in range(GROUP):
            step(pl.multiple_of((index * GROUP + inner + 1) * SUBLANES, SUBLANES))
        return carry

    if rounds > 1:
        lax.fori_loop(0, rounds, several, 0)
    done = rounds * GROUP if rounds > 1 else 0
    for index in range(done, steps):
        step((index + 1) * SUBLANES)


def edges(halo, speed_first, speed_last, force_first, force_last, thickness, own_first, own_last):
    count = speed_first.shape[0] // SUBLANES
    fields = ((speed_first, speed_last, halo), (force_first, force_last, halo - 1))
    at = 0
    for first, last, held in fields:
        for row in range(held):
            for plane in range(0, count, SUBLANES):
                start = plane * SUBLANES
                own_first[at : at + SUBLANES] = first[pl.ds(start + row, SUBLANES, stride=SUBLANES), :]
                own_last[at : at + SUBLANES] = last[pl.ds(start + SUBLANES - 1 - row, SUBLANES, stride=SUBLANES), :]
                at += SUBLANES
    spread = spread_of(thickness)
    own_first[at : at + SUBLANES] = spread
    own_last[at : at + SUBLANES] = spread


def spread_of(thickness):
    row = thickness[...]
    row = jnp.concatenate([row, jnp.zeros((1, LANES - row.shape[1]), jnp.float32)], axis=1)
    return jnp.broadcast_to(row, (SUBLANES, LANES))


def planes_of(*parts):
    return [part.at[plane] for part in parts for plane in range(part.shape[0])]


def extend_rows(rows, source, before, after, offset, held, halo, total=None, skip=0):
    count, width = len(source), source[0].shape[0]
    extended = width + 2 * halo
    for plane in range(count):
        rows[pl.ds(plane * extended + halo, width), :] = source[plane][...]
    for row in range(halo):
        for plane in range(0, count, SUBLANES):
            at = offset + row * (total or count) + skip + plane
            for edge, place in ((before, halo - 1 - row), (after, halo + width + row)):
                block = edge[pl.ds(at, SUBLANES), :] if row < held else jnp.zeros((SUBLANES, LANES), jnp.float32)
                rows[pl.ds(plane * extended + place, SUBLANES, stride=extended), :] = block


def to_tiles(rows, component, planes, tile, depth):
    extended = depth * SUBLANES
    blocks = [
        rows[pl.ds((component * planes + plane) * extended + tile, SUBLANES, stride=depth), :]
        for plane in range(planes)
    ]
    return jnp.concatenate(blocks, axis=0).T


def prepare(planes, halo, speed, force, before, after, _, speed_tiles, force_tiles, first, last, rows):
    count, width, cells = speed.shape
    depth = (width + 2 * halo) // SUBLANES
    blocks = 3 * depth
    fields = ((speed, speed_tiles, halo, 0), (force, force_tiles, halo - 1, halo * count))
    for part, (source, target, held, offset) in enumerate(fields):
        extend_rows(rows, planes_of(source), before, after, offset, held, halo)
        for component in range(3):
            for tile in range(depth):
                place = component * depth + tile
                block = to_tiles(rows, component, planes, tile, depth)
                target[place] = block
                first[part * blocks + place] = block[:halo]
                last[part * blocks + place] = block[cells - halo :]


def far_sizes(count, blocks, halo):
    rows = (2 * halo - 3) * count
    cells = -(-(2 * halo - 3) * blocks // SUBLANES) * SUBLANES
    return (0, rows, 2 * rows, 2 * rows + cells, 2 * rows + 2 * cells, 2 * rows + 2 * cells + SUBLANES)


def bundle(count, width, halo, before, after, ahead_cells, behind_cells, thickness, pack):
    blocks = ahead_cells.shape[0] // 2
    starts = far_sizes(count, blocks, halo)
    speed_rows = (halo - 1) * count
    force_rows = (halo - 2) * count
    for source, start in ((before, starts[0]), (after, starts[1])):
        pack[start : start + speed_rows] = source[:speed_rows]
        pack[start + speed_rows : start + speed_rows + force_rows] = source[halo * count : halo * count + force_rows]
    for source, start, last in ((ahead_cells, starts[2], False), (behind_cells, starts[3], True)):
        at = start
        for part, held in ((0, halo - 1), (1, halo - 2)):
            for cell in range(held):
                from_edge = halo - 1 - cell if last else cell
                for place in range(blocks):
                    pack[at : at + 1] = source[part * blocks + place, from_edge : from_edge + 1]
                    at += 1
    held = before.shape[0] - SUBLANES
    lane = lax.broadcasted_iota(jnp.int32, (SUBLANES, LANES), 1)
    spread = spread_of(thickness)
    parts = jnp.where(lane < width, before[held : held + SUBLANES], pltpu.roll(spread, width, 1))
    parts = jnp.where(lane < 2 * width, parts, pltpu.roll(after[held : held + SUBLANES], 2 * width, 1))
    pack[starts[4] : starts[5]] = parts


def hold(*refs):
    pass


def turn(block):
    lanes = lax.broadcasted_iota(jnp.int32, block.shape, 1)
    return jnp.take_along_axis(block, lanes ^ (SUBLANES - 1), axis=1)


def wrap(field):
    ring = field.shape[1] - 2 * SUBLANES
    field[:, SUBLANES - 1 : SUBLANES] = field[:, SUBLANES + ring - 1 : SUBLANES + ring]
    field[:, SUBLANES + ring : SUBLANES + ring + 1] = field[:, SUBLANES : SUBLANES + 1]


def turned_tiles(field, source, pack, part, planes, halo, rows, components=range(3)):
    count = 3 * planes
    width, cells = source[0].shape
    depth = (width + 2 * halo) // SUBLANES
    blocks = 3 * depth
    starts = far_sizes(count, blocks, halo)
    held = halo - 1 - part
    before, after = pack.at[starts[0] : starts[1]], pack.at[starts[1] : starts[2]]
    extend_rows(rows, source, before, after, part * (halo - 1) * count, held, halo, count, components[0] * planes)
    offset = part * (halo - 1) * blocks
    for number, component in enumerate(components):
        for tile in range(depth):
            block = turn(to_tiles(rows, number, planes, tile, depth))
            place = number * depth + depth - 1 - tile
            field[place, SUBLANES : SUBLANES + cells] = -block if SIGNS[component] < 0 else block
    for start, end, base, way in (
        (starts[2], starts[3], SUBLANES + cells, 1),
        (starts[3], starts[4], SUBLANES + cells + 2 * halo - 1, -1),
    ):
        edge = turn(pack[start:end])
        for cell in range(halo):
            for number, component in enumerate(components):
                for tile in range(depth):
                    place = number * depth + depth - 1 - tile
                    at = offset + cell * blocks + component * depth + tile
                    line = edge[at : at + 1] if cell < held else jnp.zeros((1, LANES), jnp.float32)
                    field[place, base + way * cell : base + way * cell + 1] = -line if SIGNS[component] < 0 else line
    wrap(field)


class Joined:
    def __init__(self, *fields):
        self.rows = [(field, place) for field in fields for place in range(field.shape[0])]

    def __getitem__(self, at):
        field, place = self.rows[at[0]]
        return field[(place,) + at[1:]]


def close_far(far_open, far_force, own_open, inside, far_residual, own, first, steps):
    depth = inside.shape[0]

    def close(start):
        at = pl.ds(start, SUBLANES)
        for place in range(far_force.shape[0]):
            now = (far_open[first + place, at, :] - far_force[place, at, :]) * inside[place % depth]
            far_residual[place, at, :] = now
            own[place, at, :] = own_open[first + place, at, :] + (0.5 * step_rate) * now

    sweep(steps, close)
    wrap(far_residual)
    wrap(own)


def row_ahead(tiles, tile):
    return tiles[tile + 1] if tile + 1 < len(tiles) else pltpu.roll(tiles[0], LANES - 1, 1)


def row_behind(tiles, tile):
    return tiles[tile - 1] if tile > 0 else pltpu.roll(tiles[-1], 1, 1)


def plane_ahead(tile):
    return pltpu.roll(tile, LANES - SUBLANES, 1)


def plane_behind(tile):
    return pltpu.roll(tile, SUBLANES, 1)


def load(field, component, depth, start):
    return [field[component * depth + tile, pl.ds(start, SUBLANES), :] for tile in range(depth)]


def residual_stage(speed, mirrored, force, thick, inside, residual, slopes, steps):
    depth = thick.shape[0]

    def step(start):
        tiles = [load(speed, component, depth, start) for component in range(3)]
        for tile in range(depth):
            thin = thick[tile]
            middle = 6.0 * thin + 0.5
            half = [0.5 * tiles[component][tile] for component in range(3)]
            for component in range(3):
                place = component * depth + tile
                here = tiles[component][tile]
                pairs = (
                    (plane_ahead(here), plane_behind(here)),
                    (row_ahead(tiles[component], tile), row_behind(tiles[component], tile)),
                    (
                        speed[place, pl.ds(start + 1, SUBLANES), :],
                        speed[place, pl.ds(start - 1, SUBLANES), :],
                    ),
                )
                around = None
                total = None
                for axis_id, (ahead, behind) in enumerate(pairs):
                    slope = ahead - behind
                    if slopes is not None:
                        slopes[axis_id * 3 * depth + place, pl.ds(start, SUBLANES), :] = slope
                    both = ahead + behind
                    around = both if around is None else around + both
                    term = half[axis_id] * slope
                    total = term if total is None else total + term
                total = total - thin * around + middle * here
                if mirrored is not None:
                    total = total - 0.5 * mirrored[place, pl.ds(start, SUBLANES), :]
                if force is not None:
                    total = total - force[place, pl.ds(start, SUBLANES), :]
                if inside is not None:
                    total = total * inside[tile]
                residual[place, pl.ds(start, SUBLANES), :] = total

    sweep(steps, step)


def descent_stage(speed, residual, mirrored, thick, inside, slopes, following, steps):
    depth = thick.shape[0]

    def step(start):
        speeds = [load(speed, component, depth, start) for component in range(3)]
        tiles = [load(residual, component, depth, start) for component in range(3)]
        rises = []
        falls = []
        for tile in range(depth):
            half = 0.5 * speeds[1][tile]
            rises.append(half + thick[tile])
            falls.append(half - thick[tile])
        upper = [[rises[tile] * tiles[c][tile] for tile in range(depth)] for c in range(3)]
        lower = [[falls[tile] * tiles[c][tile] for tile in range(depth)] for c in range(3)]
        for tile in range(depth):
            thin = thick[tile]
            flow = 0.5 * speeds[0][tile]
            flow_rise, flow_fall = flow + thin, flow - thin
            span_rise = 0.5 * speed[2 * depth + tile, pl.ds(start + 1, SUBLANES), :] + thin
            span_fall = 0.5 * speed[2 * depth + tile, pl.ds(start - 1, SUBLANES), :] - thin
            half = [0.5 * tiles[component][tile] for component in range(3)]
            middle = 6.0 * thin + 0.5
            rate = step_rate * inside[tile]
            for component in range(3):
                place = component * depth + tile
                here = tiles[component][tile]
                total = middle * here
                for inner in range(3):
                    slope = slopes[
                        (component * 3 + inner) * depth + tile, pl.ds(start, SUBLANES), :
                    ]
                    total = total + half[inner] * slope
                total = total - plane_ahead(flow_rise * here) + plane_behind(flow_fall * here)
                total = total - row_ahead(upper[component], tile) + row_behind(lower[component], tile)
                total = total - span_rise * residual[place, pl.ds(start + 1, SUBLANES), :]
                total = total + span_fall * residual[place, pl.ds(start - 1, SUBLANES), :]
                if mirrored is not None:
                    total = total - 0.5 * mirrored[place, pl.ds(start, SUBLANES), :]
                following[place, pl.ds(start, SUBLANES), :] = speeds[component][tile] - rate * total

    sweep(steps, step)


def own_part(planes, halo, wall, thickness, before, after, speed_tiles, force_tiles, ahead_cells, behind_cells,
             own, own_force, own_open, own_slopes, own_thick, inside):
    count = 3 * planes
    width = thickness.shape[1]
    cells = speed_tiles.shape[1]
    depth = own_thick.shape[0]
    blocks = 3 * depth
    for part, (field, source) in enumerate(((own, speed_tiles), (own_force, force_tiles))):
        field[:, SUBLANES : SUBLANES + cells] = source[...]
        field[:, SUBLANES + cells : SUBLANES + cells + halo] = ahead_cells[part * blocks : part * blocks + blocks]
        field[:, SUBLANES + cells + halo : SUBLANES + cells + 2 * halo] = behind_cells[part * blocks : part * blocks + blocks]
    wrap(own)
    lane = lax.broadcasted_iota(jnp.int32, (SUBLANES, LANES), 1)
    held = before.shape[0] - SUBLANES
    spread = spread_of(thickness)
    own_spread = jnp.where(lane < width, before[held : held + SUBLANES], pltpu.roll(spread, width, 1))
    own_spread = jnp.where(lane < 2 * width, own_spread, pltpu.roll(after[held : held + SUBLANES], 2 * width, 1))
    for tile in range(depth):
        row = tile - halo + depth * (lane % SUBLANES)
        own_thick[tile] = jnp.take_along_axis(own_spread, width + row, axis=1)
        row = wall[0] * width + row
        inside[tile] = jnp.where((row >= 0) & (row < wall[1] * width), 1.0, 0.0).astype(jnp.float32)
    residual_stage(own, None, own_force, own_thick, None, own_open, own_slopes, (cells + 2 * halo) // SUBLANES)


def before_force(planes, halo, partner_1, partner_2, pack, own, own_partial, own_slopes, own_thick, inside,
                 far, own_residual, far_open, own_open, far_slopes, far_thick, far_force, far_residual, own_next,
                 rows):
    count = 3 * planes
    _, width, cells = partner_1.shape
    depth = own_thick.shape[0]
    blocks = 3 * depth
    lane = lax.broadcasted_iota(jnp.int32, (SUBLANES, LANES), 1)
    starts = far_sizes(count, blocks, halo)
    far_spread = pack[starts[4] : starts[5]]
    for tile in range(depth):
        row = tile - halo + depth * (lane % SUBLANES)
        far_thick[tile] = jnp.take_along_axis(far_spread, 2 * width - 1 - row, axis=1)
    turned_tiles(far, planes_of(partner_1), pack, 0, planes, halo, rows)
    steps = (cells + 2 * halo) // SUBLANES

    def close(start):
        at = pl.ds(start, SUBLANES)
        for place in range(blocks):
            own_residual[place, at, :] = (own_partial[place, at, :] - 0.5 * far[place, at, :]) * inside[place % depth]

    sweep(steps, close)
    wrap(own_residual)
    residual_stage(far, own, None, far_thick, None, far_open, far_slopes, steps)
    descent_stage(own, own_residual, None, own_thick, inside, own_slopes, own_open, steps)
    turned_tiles(far_force, planes_of(partner_2), pack, 1, planes, halo, rows, range(2))
    close_far(far_open, far_force, own_open, inside, far_residual, own_next, 0, steps)


def with_force(planes, halo, partner_3, pack,
               own_force, own_thick, inside, far, own_residual, far_open, own_open, far_slopes, far_thick,
               far_force_1, far_residual_1, own_1,
               speed_out, residual_out,
               speed_buffer, residual_buffer, sems, rows, far_force_2, far_residual_2, own_2,
               far_mirror, next_residual, next_own, next_far, own_slopes):
    count = 3 * planes
    _, width, cells = partner_3.shape
    depth = own_thick.shape[0]
    steps = (cells + 2 * halo) // SUBLANES
    turned_tiles(far_force_2, planes_of(partner_3), pack, 1, planes, halo, rows, range(2, 3))
    close_far(far_open, far_force_2, own_open, inside, far_residual_2, own_2, 2 * depth, steps)
    far_force = Joined(far_force_1, far_force_2)
    far_residual = Joined(far_residual_1, far_residual_2)
    own = Joined(own_1, own_2)
    descent_stage(far, far_residual, own_residual, far_thick, inside, far_slopes, next_far, steps)
    wrap(next_far)
    far = next_far
    residual_stage(own, far, own_force, own_thick, inside, next_residual, own_slopes, steps)
    wrap(next_residual)
    residual_copies = send_out(next_residual, residual_buffer, residual_out, sems.at[0], rows, planes, depth, halo)
    residual_stage(far, own, far_force, far_thick, inside, far_mirror, None, cells // SUBLANES)
    descent_stage(own, next_residual, far_mirror, own_thick, inside, own_slopes, next_own, cells // SUBLANES)
    speed_copies = send_out(next_own, speed_buffer, speed_out, sems.at[1], rows, planes, depth, halo)
    for copy in residual_copies + speed_copies:
        copy.wait()


def send_out(field, buffer, target, sems, rows, planes, depth, halo):
    _, width, cells = buffer.shape
    extended = depth * SUBLANES
    copies = []
    for component in range(3):
        for tile in range(depth):
            block = field[component * depth + tile, SUBLANES : SUBLANES + cells].T
            for plane in range(planes):
                at = (component * planes + plane) * extended + tile
                rows[pl.ds(at, SUBLANES, stride=depth), :] = block[plane * SUBLANES : (plane + 1) * SUBLANES]
        for plane in range(component * planes, (component + 1) * planes):
            buffer[plane] = rows[pl.ds(plane * extended + halo, width), :]
        part = pl.ds(component * planes, planes)
        copies.append(pltpu.make_async_copy(buffer.at[part], target.at[part], sems.at[component]))
        copies[-1].start()
    return copies


def carried(starting_speed_vector, driving_source, viscosity):
    shape = starting_speed_vector.shape
    _, _, planes, width, cells = shape
    halo = 2 * ITERS
    depth = (width + 2 * halo) // SUBLANES
    blocks = 3 * depth
    count = 3 * planes
    whole = pl.BlockSpec(memory_space=pltpu.VMEM)
    arrays = lambda *sizes: jax.ShapeDtypeStruct(sizes, jnp.float32)
    grant = lambda mega: pltpu.CompilerParams(vmem_limit_bytes=mega * 2**20)
    tall = cells + 2 * halo + 2 * SUBLANES
    rows = pltpu.VMEM((count * (width + 2 * halo), cells), jnp.float32)
    field = pltpu.VMEM((blocks, tall, LANES), jnp.float32)
    slope = pltpu.VMEM((3 * blocks, tall, LANES), jnp.float32)
    speed = starting_speed_vector.reshape(count, width, cells)
    force = driving_source.reshape(count, width, cells)

    walls, spans = lax.axis_size("wall"), lax.axis_size("span")
    upward = [(i, i + 1) for i in range(walls - 1)]
    downward = [(i + 1, i) for i in range(walls - 1)]
    onward = [(i, (i + 1) % spans) for i in range(spans)]
    backward = [((i + 1) % spans, i) for i in range(spans)]
    to_partner = functools.partial(lax.ppermute, axis_name=("tm", "wall"), perm=partner_pairs())

    cut = 2 * planes
    partner_1 = to_partner(speed)
    sent_2 = force[:cut]
    sent_3 = force[cut:]
    any_place = pl.BlockSpec(memory_space=pl.ANY)
    after_all = lambda held, *others: pl.pallas_call(
        hold,
        out_shape=arrays(*held.shape),
        in_specs=[any_place] * (1 + len(others)),
        out_specs=any_place,
        input_output_aliases={0: 0},
        compiler_params=grant(1),
        name="hold",
    )(held, *others)

    thickness = viscosity.reshape(1, width)
    tops = pl.BlockSpec((count, SUBLANES, cells), lambda i: (0, 0, 0))
    ends = pl.BlockSpec((count, SUBLANES, cells), lambda i: (0, width // SUBLANES - 1, 0))
    lines = (2 * halo - 1) * count + SUBLANES
    flat = lambda ref: ref.reshape(count * SUBLANES, cells)
    own_first, own_last = pl.pallas_call(
        lambda a, b, c, d, *rest: edges(halo, flat(a), flat(b), flat(c), flat(d), *rest),
        out_shape=(arrays(lines, cells),) * 2,
        grid=(1,),
        in_specs=[tops, ends, tops, ends, pl.BlockSpec((1, width), lambda i: (0, 0))],
        out_specs=[pl.BlockSpec((lines, cells), lambda i: (0, 0))] * 2,
        compiler_params=grant(8),
        name="edges",
    )(speed, speed, force, force, thickness)
    before = lax.ppermute(own_last, "wall", upward)
    after = lax.ppermute(own_first, "wall", downward)
    partner_2 = to_partner(after_all(sent_2, before, after))
    speed_tiles, force_tiles, first, last = pl.pallas_call(
        functools.partial(prepare, planes, halo),
        out_shape=(arrays(blocks, cells, LANES),) * 2 + (arrays(2 * blocks, halo, LANES),) * 2,
        in_specs=[whole] * 4 + [any_place],
        out_specs=[whole] * 4,
        scratch_shapes=[rows],
        compiler_params=grant(8),
        name="prepare",
    )(speed, force, before, after, partner_1)
    behind_cells = lax.ppermute(last, "span", onward)
    ahead_cells = lax.ppermute(first, "span", backward)
    pack = pl.pallas_call(
        functools.partial(bundle, count, width, halo),
        out_shape=arrays(far_sizes(count, blocks, halo)[-1], LANES),
        in_specs=[whole] * 5,
        out_specs=whole,
        compiler_params=grant(8),
        name="bundle",
    )(before, after, ahead_cells, behind_cells, thickness)
    far_pack = to_partner(pack)
    partner_3 = to_partner(after_all(sent_3, pack, partner_2))

    wall = jnp.stack([lax.axis_index("wall"), jnp.int32(walls)])
    own, own_force, own_partial, own_slopes, own_thick, inside = pl.pallas_call(
        functools.partial(own_part, planes, halo),
        out_shape=(arrays(blocks, tall, LANES),) * 3
        + (arrays(3 * blocks, tall, LANES),)
        + (arrays(depth, SUBLANES, LANES),) * 2,
        in_specs=[pl.BlockSpec(memory_space=pltpu.SMEM)] + [whole] * 7,
        out_specs=[whole] * 6,
        compiler_params=grant(14),
        name="own_part",
    )(wall, thickness, before, after, speed_tiles, force_tiles, ahead_cells, behind_cells)
    early = pl.pallas_call(
        functools.partial(before_force, planes, halo),
        out_shape=(arrays(blocks, tall, LANES),) * 4
        + (arrays(3 * blocks, tall, LANES), arrays(depth, SUBLANES, LANES))
        + (arrays(2 * depth, tall, LANES),) * 3,
        in_specs=[whole] * 8,
        out_specs=[whole] * 9,
        scratch_shapes=[rows],
        compiler_params=grant(20),
        name="before_force",
    )(partner_1, partner_2, far_pack, own, own_partial, own_slopes, own_thick, inside)
    out = pltpu.VMEM((count, width, cells), jnp.float32)
    speed_out, residual_out = pl.pallas_call(
        functools.partial(with_force, planes, halo),
        out_shape=(arrays(count, width, cells), arrays(count, width, cells)),
        in_specs=[whole] * 14,
        out_specs=[any_place] * 2,
        scratch_shapes=[out, out, pltpu.SemaphoreType.DMA((2, 3)), rows]
        + [pltpu.VMEM((depth, tall, LANES), jnp.float32)] * 3
        + [field] * 4
        + [slope],
        compiler_params=grant(30),
        name="with_force",
    )(partner_3, far_pack, own_force, own_thick, inside, *early)
    return speed_out.reshape(shape), residual_out.reshape(shape)


def local(starting_speed_vector, driving_source, viscosity):
    _, instants, planes, width, cells = starting_speed_vector.shape
    times = lax.axis_size("tm") * instants
    halo = 2 * ITERS
    one_instant = ITERS == 2 and instants == 1 and not instant_weights(times)
    tiled = planes * SUBLANES == LANES and cells == LANES and (width + 2 * halo) % SUBLANES == 0
    rows_fit = halo <= width and 3 * width <= LANES and (2 * halo) % SUBLANES == 0
    if one_instant and tiled and rows_fit:
        return carried(starting_speed_vector, driving_source, viscosity)
    return staged(starting_speed_vector, driving_source, viscosity)


def solution(mesh):
    placed = (P(None, "tm", None, "wall", "span"), P(None, "tm", None, "wall", "span"), P("wall"))
    return jax.shard_map(
        local,
        mesh=mesh,
        in_specs=placed,
        out_specs=(P(None, "tm", None, "wall", "span"), P(None, "tm", None, "wall", "span")),
        check_vma=False,
    )
```

```python
import functools

import jax
import jax.numpy as jnp
from jax import lax
from jax.experimental import pallas as pl
from jax.experimental.pallas import tpu as pltpu
from jax.sharding import PartitionSpec as P

ITERS = 2


step_rate = 0.05
LANES = 128
SUBLANES = 8
SIGNS = (1.0, -1.0, 1.0)


def instant_weights(instants):
    weights = {}
    for offset, weight in ((1, 0.5), (-1, -0.5)):
        weights[offset % instants] = weights.get(offset % instants, 0.0) + weight
    return {offset: weight for offset, weight in weights.items() if weight != 0.0}


def with_halo(cells, sides, width, closed):
    for axis, dim in sides:
        count = lax.axis_size(axis)
        ends = count if closed else count - 1
        head = lax.slice_in_dim(cells, 0, width, axis=dim)
        tail = lax.slice_in_dim(cells, cells.shape[dim] - width, cells.shape[dim], axis=dim)
        cells = jnp.concatenate(
            [
                lax.ppermute(tail, axis, [(i, (i + 1) % count) for i in range(ends)]),
                cells,
                lax.ppermute(head, axis, [((i + 1) % count, i) for i in range(ends)]),
            ],
            axis=dim,
        )
    return cells


def time_slope(values):
    instants = values.shape[1] * lax.axis_size("tm")
    if not instant_weights(instants):
        return jnp.zeros_like(values)
    padded_state = with_halo(values, (("tm", 1),), 1, True)
    return 0.5 * (padded_state[:, 2:] - padded_state[:, :-2])


def wall_pair(values):
    padded_state = with_halo(values, (("wall", 3),), 1, False)
    return (padded_state[:, :, :, 2:], padded_state[:, :, :, :-2])


def span_pair(values):
    padded_state = with_halo(values, (("span", 4),), 1, True)
    return (padded_state[:, :, :, :, 2:], padded_state[:, :, :, :, :-2])


def along_flow(values):
    return (jnp.roll(values, -1, 2), jnp.roll(values, 1, 2))


def partner_pairs():
    times, walls = lax.axis_size("tm"), lax.axis_size("wall")
    return [
        (time * walls + wall, ((time + times // 2) % times) * walls + walls - 1 - wall)
        for time in range(times)
        for wall in range(walls)
    ]


def reflect(values):
    sign_row = jnp.array(SIGNS, jnp.float32).reshape(3, 1, 1, 1, 1)
    partner = lax.ppermute(values, ("tm", "wall"), partner_pairs())
    return partner[:, :, :, ::-1, :] * sign_row


def residual_of(present_state, mirrored, driving_source, viscous):
    neighbours = (along_flow(present_state), wall_pair(present_state), span_pair(present_state))
    slopes = [0.5 * (ahead - behind) for ahead, behind in neighbours]
    advect = (
        present_state[0:1] * slopes[0]
        + present_state[1:2] * slopes[1]
        + present_state[2:3] * slopes[2]
    )
    laplace = neighbours[0][0] + neighbours[0][1] - 2.0 * present_state
    laplace = laplace + (neighbours[1][0] + neighbours[1][1] - 2.0 * present_state)
    laplace = laplace + (neighbours[2][0] + neighbours[2][1] - 2.0 * present_state)
    residual_now = (
        time_slope(present_state)
        + advect
        - viscous * laplace
        + 0.5 * (present_state - mirrored)
        - driving_source
    )
    return (residual_now, neighbours, slopes)


def descent_part(neighbours, slopes, residual_now, viscous):
    scaled = viscous * residual_now
    wall_ahead, wall_behind = wall_pair(jnp.concatenate((residual_now, scaled), 0))
    flow_ahead, flow_behind = along_flow(residual_now)
    span_ahead, span_behind = span_pair(residual_now)
    residual_pairs = (
        (flow_ahead, flow_behind),
        (wall_ahead[:3], wall_behind[:3]),
        (span_ahead, span_behind),
    )
    transport = jnp.stack(
        [jnp.sum(residual_now * slopes[component], axis=0) for component in range(3)]
    )
    second = None
    for axis_id in range(3):
        ahead_u = neighbours[axis_id][0][axis_id : axis_id + 1]
        behind_u = neighbours[axis_id][1][axis_id : axis_id + 1]
        term = 0.5 * (ahead_u * residual_pairs[axis_id][0] - behind_u * residual_pairs[axis_id][1])
        second = term if second is None else second + term
    diffused = viscous * flow_ahead + viscous * flow_behind - 2.0 * scaled
    diffused = diffused + (wall_ahead[3:] + wall_behind[3:] - 2.0 * scaled)
    diffused = diffused + (viscous * span_ahead + viscous * span_behind - 2.0 * scaled)
    return -time_slope(residual_now) + transport - second - diffused


def staged(starting_speed_vector, driving_source, viscosity):
    viscous = viscosity[None, None, None, :, None]
    present_state = starting_speed_vector
    residual_now = starting_speed_vector
    for iteration in range(ITERS):
        mirrored = reflect(present_state)
        residual_now, neighbours, slopes = residual_of(
            present_state, mirrored, driving_source, viscous
        )
        local_part = descent_part(neighbours, slopes, residual_now, viscous)
        mirror_residual = reflect(residual_now)
        present_state = present_state - step_rate * (
            local_part + 0.5 * (residual_now - mirror_residual)
        )
    return (present_state, residual_now)


GROUP = 17


def sweep(steps, step):
    rounds = steps // GROUP

    def several(index, carry):
        for inner in range(GROUP):
            step(pl.multiple_of((index * GROUP + inner + 1) * SUBLANES, SUBLANES))
        return carry

    if rounds > 1:
        lax.fori_loop(0, rounds, several, 0)
    done = rounds * GROUP if rounds > 1 else 0
    for index in range(done, steps):
        step((index + 1) * SUBLANES)


def edges(halo, speed_first, speed_last, force_first, force_last, thickness, own_first, own_last):
    count = speed_first.shape[0] // SUBLANES
    fields = ((speed_first, speed_last, halo), (force_first, force_last, halo - 1))
    at = 0
    for first, last, held in fields:
        for row in range(held):
            for plane in range(0, count, SUBLANES):
                start = plane * SUBLANES
                own_first[at : at + SUBLANES] = first[pl.ds(start + row, SUBLANES, stride=SUBLANES), :]
                own_last[at : at + SUBLANES] = last[pl.ds(start + SUBLANES - 1 - row, SUBLANES, stride=SUBLANES), :]
                at += SUBLANES
    spread = spread_of(thickness)
    own_first[at : at + SUBLANES] = spread
    own_last[at : at + SUBLANES] = spread


def spread_of(thickness):
    row = thickness[...]
    row = jnp.concatenate([row, jnp.zeros((1, LANES - row.shape[1]), jnp.float32)], axis=1)
    return jnp.broadcast_to(row, (SUBLANES, LANES))


def planes_of(*parts):
    return [part.at[plane] for part in parts for plane in range(part.shape[0])]


def extend_rows(rows, source, before, after, offset, held, halo, total=None, skip=0):
    count, width = len(source), source[0].shape[0]
    extended = width + 2 * halo
    for plane in range(count):
        rows[pl.ds(plane * extended + halo, width), :] = source[plane][...]
    for row in range(halo):
        for plane in range(0, count, SUBLANES):
            at = offset + row * (total or count) + skip + plane
            for edge, place in ((before, halo - 1 - row), (after, halo + width + row)):
                block = edge[pl.ds(at, SUBLANES), :] if row < held else jnp.zeros((SUBLANES, LANES), jnp.float32)
                rows[pl.ds(plane * extended + place, SUBLANES, stride=extended), :] = block


def to_tiles(rows, component, planes, tile, depth):
    extended = depth * SUBLANES
    blocks = [
        rows[pl.ds((component * planes + plane) * extended + tile, SUBLANES, stride=depth), :]
        for plane in range(planes)
    ]
    return jnp.concatenate(blocks, axis=0).T


def tile_fields(planes, halo, speed, force, before, after, rows):
    count, width, _ = speed.shape
    depth = (width + 2 * halo) // SUBLANES
    for part, (source, held, offset) in enumerate(((speed, halo, 0), (force, halo - 1, halo * count))):
        extend_rows(rows, planes_of(source), before, after, offset, held, halo)
        for component in range(3):
            for tile in range(depth):
                yield (part * 3 + component) * depth + tile, to_tiles(rows, component, planes, tile, depth)


def edge_cells(planes, halo, speed, force, before, after, _, first, last, rows):
    cells = speed.shape[-1]
    for place, block in tile_fields(planes, halo, speed, force, before, after, rows):
        first[place] = block[:halo]
        last[place] = block[cells - halo :]


def own_tiles(planes, halo, speed, force, before, after, _, speed_tiles, force_tiles, rows):
    blocks = speed_tiles.shape[0]
    for place, block in tile_fields(planes, halo, speed, force, before, after, rows):
        (speed_tiles if place < blocks else force_tiles)[place % blocks] = block


def far_sizes(count, blocks, halo):
    rows = (2 * halo - 3) * count
    cells = -(-(2 * halo - 3) * blocks // SUBLANES) * SUBLANES
    return (0, rows, 2 * rows, 2 * rows + cells, 2 * rows + 2 * cells, 2 * rows + 2 * cells + SUBLANES)


def bundle(count, width, halo, before, after, ahead_cells, behind_cells, thickness, _, pack):
    blocks = ahead_cells.shape[0] // 2
    starts = far_sizes(count, blocks, halo)
    speed_rows = (halo - 1) * count
    force_rows = (halo - 2) * count
    for source, start in ((before, starts[0]), (after, starts[1])):
        pack[start : start + speed_rows] = source[:speed_rows]
        pack[start + speed_rows : start + speed_rows + force_rows] = source[halo * count : halo * count + force_rows]
    for source, start, last in ((ahead_cells, starts[2], False), (behind_cells, starts[3], True)):
        at = start
        for part, held in ((0, halo - 1), (1, halo - 2)):
            for cell in range(held):
                from_edge = halo - 1 - cell if last else cell
                for place in range(blocks):
                    pack[at : at + 1] = source[part * blocks + place, from_edge : from_edge + 1]
                    at += 1
    held = before.shape[0] - SUBLANES
    lane = lax.broadcasted_iota(jnp.int32, (SUBLANES, LANES), 1)
    spread = spread_of(thickness)
    parts = jnp.where(lane < width, before[held : held + SUBLANES], pltpu.roll(spread, width, 1))
    parts = jnp.where(lane < 2 * width, parts, pltpu.roll(after[held : held + SUBLANES], 2 * width, 1))
    pack[starts[4] : starts[5]] = parts


def hold(*refs):
    pass


def turn(block):
    lanes = lax.broadcasted_iota(jnp.int32, block.shape, 1)
    return jnp.take_along_axis(block, lanes ^ (SUBLANES - 1), axis=1)


def wrap(field):
    ring = field.shape[1] - 2 * SUBLANES
    field[:, SUBLANES - 1 : SUBLANES] = field[:, SUBLANES + ring - 1 : SUBLANES + ring]
    field[:, SUBLANES + ring : SUBLANES + ring + 1] = field[:, SUBLANES : SUBLANES + 1]


def turned_tiles(field, source, pack, part, planes, halo, rows, components=range(3)):
    count = 3 * planes
    width, cells = source[0].shape
    depth = (width + 2 * halo) // SUBLANES
    blocks = 3 * depth
    starts = far_sizes(count, blocks, halo)
    held = halo - 1 - part
    before, after = pack.at[starts[0] : starts[1]], pack.at[starts[1] : starts[2]]
    extend_rows(rows, source, before, after, part * (halo - 1) * count, held, halo, count, components[0] * planes)
    offset = part * (halo - 1) * blocks
    for number, component in enumerate(components):
        for tile in range(depth):
            block = turn(to_tiles(rows, number, planes, tile, depth))
            place = number * depth + depth - 1 - tile
            field[place, SUBLANES : SUBLANES + cells] = -block if SIGNS[component] < 0 else block
    for start, end, base, way in (
        (starts[2], starts[3], SUBLANES + cells, 1),
        (starts[3], starts[4], SUBLANES + cells + 2 * halo - 1, -1),
    ):
        edge = turn(pack[start:end])
        for cell in range(halo):
            for number, component in enumerate(components):
                for tile in range(depth):
                    place = number * depth + depth - 1 - tile
                    at = offset + cell * blocks + component * depth + tile
                    line = edge[at : at + 1] if cell < held else jnp.zeros((1, LANES), jnp.float32)
                    field[place, base + way * cell : base + way * cell + 1] = -line if SIGNS[component] < 0 else line
    wrap(field)


class Joined:
    def __init__(self, *fields):
        self.rows = [(field, place) for field in fields for place in range(field.shape[0])]

    def __getitem__(self, at):
        field, place = self.rows[at[0]]
        return field[(place,) + at[1:]]


def close_far(far_open, far_force, own_open, inside, far_residual, own, first, steps):
    depth = inside.shape[0]

    def close(start):
        at = pl.ds(start, SUBLANES)
        for place in range(far_force.shape[0]):
            now = (far_open[first + place, at, :] - far_force[place, at, :]) * inside[place % depth]
            far_residual[place, at, :] = now
            own[place, at, :] = own_open[first + place, at, :] + (0.5 * step_rate) * now

    sweep(steps, close)
    wrap(far_residual)
    wrap(own)


def row_ahead(tiles, tile):
    return tiles[tile + 1] if tile + 1 < len(tiles) else pltpu.roll(tiles[0], LANES - 1, 1)


def row_behind(tiles, tile):
    return tiles[tile - 1] if tile > 0 else pltpu.roll(tiles[-1], 1, 1)


def plane_ahead(tile):
    return pltpu.roll(tile, LANES - SUBLANES, 1)


def plane_behind(tile):
    return pltpu.roll(tile, SUBLANES, 1)


def load(field, component, depth, start):
    return [field[component * depth + tile, pl.ds(start, SUBLANES), :] for tile in range(depth)]


def residual_stage(speed, mirrored, force, thick, inside, residual, slopes, steps):
    depth = thick.shape[0]

    def step(start):
        tiles = [load(speed, component, depth, start) for component in range(3)]
        for tile in range(depth):
            thin = thick[tile]
            middle = 6.0 * thin + 0.5
            half = [0.5 * tiles[component][tile] for component in range(3)]
            for component in range(3):
                place = component * depth + tile
                here = tiles[component][tile]
                pairs = (
                    (plane_ahead(here), plane_behind(here)),
                    (row_ahead(tiles[component], tile), row_behind(tiles[component], tile)),
                    (
                        speed[place, pl.ds(start + 1, SUBLANES), :],
                        speed[place, pl.ds(start - 1, SUBLANES), :],
                    ),
                )
                around = None
                total = None
                for axis_id, (ahead, behind) in enumerate(pairs):
                    slope = ahead - behind
                    if slopes is not None:
                        slopes[axis_id * 3 * depth + place, pl.ds(start, SUBLANES), :] = slope
                    both = ahead + behind
                    around = both if around is None else around + both
                    term = half[axis_id] * slope
                    total = term if total is None else total + term
                total = total - thin * around + middle * here
                if mirrored is not None:
                    total = total - 0.5 * mirrored[place, pl.ds(start, SUBLANES), :]
                if force is not None:
                    total = total - force[place, pl.ds(start, SUBLANES), :]
                if inside is not None:
                    total = total * inside[tile]
                residual[place, pl.ds(start, SUBLANES), :] = total

    sweep(steps, step)


def descent_stage(speed, residual, mirrored, thick, inside, slopes, following, steps):
    depth = thick.shape[0]

    def step(start):
        speeds = [load(speed, component, depth, start) for component in range(3)]
        tiles = [load(residual, component, depth, start) for component in range(3)]
        rises = []
        falls = []
        for tile in range(depth):
            half = 0.5 * speeds[1][tile]
            rises.append(half + thick[tile])
            falls.append(half - thick[tile])
        upper = [[rises[tile] * tiles[c][tile] for tile in range(depth)] for c in range(3)]
        lower = [[falls[tile] * tiles[c][tile] for tile in range(depth)] for c in range(3)]
        for tile in range(depth):
            thin = thick[tile]
            flow = 0.5 * speeds[0][tile]
            flow_rise, flow_fall = flow + thin, flow - thin
            span_rise = 0.5 * speed[2 * depth + tile, pl.ds(start + 1, SUBLANES), :] + thin
            span_fall = 0.5 * speed[2 * depth + tile, pl.ds(start - 1, SUBLANES), :] - thin
            half = [0.5 * tiles[component][tile] for component in range(3)]
            middle = 6.0 * thin + 0.5
            rate = step_rate * inside[tile]
            for component in range(3):
                place = component * depth + tile
                here = tiles[component][tile]
                total = middle * here
                for inner in range(3):
                    slope = slopes[
                        (component * 3 + inner) * depth + tile, pl.ds(start, SUBLANES), :
                    ]
                    total = total + half[inner] * slope
                total = total - plane_ahead(flow_rise * here) + plane_behind(flow_fall * here)
                total = total - row_ahead(upper[component], tile) + row_behind(lower[component], tile)
                total = total - span_rise * residual[place, pl.ds(start + 1, SUBLANES), :]
                total = total + span_fall * residual[place, pl.ds(start - 1, SUBLANES), :]
                if mirrored is not None:
                    total = total - 0.5 * mirrored[place, pl.ds(start, SUBLANES), :]
                following[place, pl.ds(start, SUBLANES), :] = speeds[component][tile] - rate * total

    sweep(steps, step)


def own_part(planes, halo, wall, thickness, before, after, speed_tiles, force_tiles, ahead_cells, behind_cells,
             own, own_force, own_open, own_slopes, own_thick, inside):
    count = 3 * planes
    width = thickness.shape[1]
    cells = speed_tiles.shape[1]
    depth = own_thick.shape[0]
    blocks = 3 * depth
    for part, (field, source) in enumerate(((own, speed_tiles), (own_force, force_tiles))):
        field[:, SUBLANES : SUBLANES + cells] = source[...]
        field[:, SUBLANES + cells : SUBLANES + cells + halo] = ahead_cells[part * blocks : part * blocks + blocks]
        field[:, SUBLANES + cells + halo : SUBLANES + cells + 2 * halo] = behind_cells[part * blocks : part * blocks + blocks]
    wrap(own)
    lane = lax.broadcasted_iota(jnp.int32, (SUBLANES, LANES), 1)
    held = before.shape[0] - SUBLANES
    spread = spread_of(thickness)
    own_spread = jnp.where(lane < width, before[held : held + SUBLANES], pltpu.roll(spread, width, 1))
    own_spread = jnp.where(lane < 2 * width, own_spread, pltpu.roll(after[held : held + SUBLANES], 2 * width, 1))
    for tile in range(depth):
        row = tile - halo + depth * (lane % SUBLANES)
        own_thick[tile] = jnp.take_along_axis(own_spread, width + row, axis=1)
        row = wall[0] * width + row
        inside[tile] = jnp.where((row >= 0) & (row < wall[1] * width), 1.0, 0.0).astype(jnp.float32)
    residual_stage(own, None, own_force, own_thick, None, own_open, own_slopes, (cells + 2 * halo) // SUBLANES)


def before_force(planes, halo, partner_1, partner_2, pack, own, own_partial, own_slopes, own_thick, inside,
                 far, own_residual, far_open, own_open, far_slopes, far_thick, far_force, far_residual, own_next,
                 rows):
    count = 3 * planes
    _, width, cells = partner_1.shape
    depth = own_thick.shape[0]
    blocks = 3 * depth
    lane = lax.broadcasted_iota(jnp.int32, (SUBLANES, LANES), 1)
    starts = far_sizes(count, blocks, halo)
    far_spread = pack[starts[4] : starts[5]]
    for tile in range(depth):
        row = tile - halo + depth * (lane % SUBLANES)
        far_thick[tile] = jnp.take_along_axis(far_spread, 2 * width - 1 - row, axis=1)
    turned_tiles(far, planes_of(partner_1), pack, 0, planes, halo, rows)
    steps = (cells + 2 * halo) // SUBLANES

    def close(start):
        at = pl.ds(start, SUBLANES)
        for place in range(blocks):
            own_residual[place, at, :] = (own_partial[place, at, :] - 0.5 * far[place, at, :]) * inside[place % depth]

    sweep(steps, close)
    wrap(own_residual)
    residual_stage(far, own, None, far_thick, None, far_open, far_slopes, steps)
    descent_stage(own, own_residual, None, own_thick, inside, own_slopes, own_open, steps)
    turned_tiles(far_force, planes_of(partner_2), pack, 1, planes, halo, rows, range(2))
    close_far(far_open, far_force, own_open, inside, far_residual, own_next, 0, steps)


def with_force(planes, halo, partner_3, pack,
               own_force, own_thick, inside, far, own_residual, far_open, own_open, far_slopes, far_thick,
               far_force_1, far_residual_1, own_1,
               speed_out, residual_out,
               speed_buffer, residual_buffer, sems, rows, far_force_2, far_residual_2, own_2,
               far_mirror, next_residual, next_own, next_far, own_slopes):
    count = 3 * planes
    _, width, cells = partner_3.shape
    depth = own_thick.shape[0]
    steps = (cells + 2 * halo) // SUBLANES
    turned_tiles(far_force_2, planes_of(partner_3), pack, 1, planes, halo, rows, range(2, 3))
    close_far(far_open, far_force_2, own_open, inside, far_residual_2, own_2, 2 * depth, steps)
    far_force = Joined(far_force_1, far_force_2)
    far_residual = Joined(far_residual_1, far_residual_2)
    own = Joined(own_1, own_2)
    descent_stage(far, far_residual, own_residual, far_thick, inside, far_slopes, next_far, steps)
    wrap(next_far)
    far = next_far
    residual_stage(own, far, own_force, own_thick, inside, next_residual, own_slopes, steps)
    wrap(next_residual)
    residual_copies = send_out(next_residual, residual_buffer, residual_out, sems.at[0], rows, planes, depth, halo)
    residual_stage(far, own, far_force, far_thick, inside, far_mirror, None, cells // SUBLANES)
    descent_stage(own, next_residual, far_mirror, own_thick, inside, own_slopes, next_own, cells // SUBLANES)
    speed_copies = send_out(next_own, speed_buffer, speed_out, sems.at[1], rows, planes, depth, halo)
    for copy in residual_copies + speed_copies:
        copy.wait()


def send_out(field, buffer, target, sems, rows, planes, depth, halo):
    _, width, cells = buffer.shape
    extended = depth * SUBLANES
    copies = []
    for component in range(3):
        for tile in range(depth):
            block = field[component * depth + tile, SUBLANES : SUBLANES + cells].T
            for plane in range(planes):
                at = (component * planes + plane) * extended + tile
                rows[pl.ds(at, SUBLANES, stride=depth), :] = block[plane * SUBLANES : (plane + 1) * SUBLANES]
        for plane in range(component * planes, (component + 1) * planes):
            buffer[plane] = rows[pl.ds(plane * extended + halo, width), :]
        part = pl.ds(component * planes, planes)
        copies.append(pltpu.make_async_copy(buffer.at[part], target.at[part], sems.at[component]))
        copies[-1].start()
    return copies


def carried(starting_speed_vector, driving_source, viscosity):
    shape = starting_speed_vector.shape
    _, _, planes, width, cells = shape
    halo = 2 * ITERS
    depth = (width + 2 * halo) // SUBLANES
    blocks = 3 * depth
    count = 3 * planes
    whole = pl.BlockSpec(memory_space=pltpu.VMEM)
    arrays = lambda *sizes: jax.ShapeDtypeStruct(sizes, jnp.float32)
    grant = lambda mega: pltpu.CompilerParams(vmem_limit_bytes=mega * 2**20)
    tall = cells + 2 * halo + 2 * SUBLANES
    rows = pltpu.VMEM((count * (width + 2 * halo), cells), jnp.float32)
    field = pltpu.VMEM((blocks, tall, LANES), jnp.float32)
    slope = pltpu.VMEM((3 * blocks, tall, LANES), jnp.float32)
    speed = starting_speed_vector.reshape(count, width, cells)
    force = driving_source.reshape(count, width, cells)

    walls, spans = lax.axis_size("wall"), lax.axis_size("span")
    upward = [(i, i + 1) for i in range(walls - 1)]
    downward = [(i + 1, i) for i in range(walls - 1)]
    onward = [(i, (i + 1) % spans) for i in range(spans)]
    backward = [((i + 1) % spans, i) for i in range(spans)]
    to_partner = functools.partial(lax.ppermute, axis_name=("tm", "wall"), perm=partner_pairs())

    cut = 2 * planes
    partner_1 = to_partner(speed)
    sent_2 = force[:cut]
    sent_3 = force[cut:]
    any_place = pl.BlockSpec(memory_space=pl.ANY)
    after_all = lambda held, *others: pl.pallas_call(
        hold,
        out_shape=arrays(*held.shape),
        in_specs=[any_place] * (1 + len(others)),
        out_specs=any_place,
        input_output_aliases={0: 0},
        compiler_params=grant(1),
        name="hold",
    )(held, *others)

    thickness = viscosity.reshape(1, width)
    tops = pl.BlockSpec((count, SUBLANES, cells), lambda i: (0, 0, 0))
    ends = pl.BlockSpec((count, SUBLANES, cells), lambda i: (0, width // SUBLANES - 1, 0))
    lines = (2 * halo - 1) * count + SUBLANES
    flat = lambda ref: ref.reshape(count * SUBLANES, cells)
    own_first, own_last = pl.pallas_call(
        lambda a, b, c, d, *rest: edges(halo, flat(a), flat(b), flat(c), flat(d), *rest),
        out_shape=(arrays(lines, cells),) * 2,
        grid=(1,),
        in_specs=[tops, ends, tops, ends, pl.BlockSpec((1, width), lambda i: (0, 0))],
        out_specs=[pl.BlockSpec((lines, cells), lambda i: (0, 0))] * 2,
        compiler_params=grant(8),
        name="edges",
    )(speed, speed, force, force, thickness)
    before = lax.ppermute(own_last, "wall", upward)
    after = lax.ppermute(own_first, "wall", downward)
    partner_2 = to_partner(after_all(sent_2, before, after))
    first, last = pl.pallas_call(
        functools.partial(edge_cells, planes, halo),
        out_shape=(arrays(2 * blocks, halo, LANES),) * 2,
        in_specs=[whole] * 4 + [any_place],
        out_specs=[whole] * 2,
        scratch_shapes=[rows],
        compiler_params=grant(8),
        name="edge_cells",
    )(speed, force, before, after, partner_1)
    speed_tiles, force_tiles = pl.pallas_call(
        functools.partial(own_tiles, planes, halo),
        out_shape=(arrays(blocks, cells, LANES),) * 2,
        in_specs=[whole] * 4 + [any_place],
        out_specs=[whole] * 2,
        scratch_shapes=[rows],
        compiler_params=grant(8),
        name="own_tiles",
    )(speed, force, before, after, first)
    behind_cells = lax.ppermute(last, "span", onward)
    ahead_cells = lax.ppermute(first, "span", backward)
    pack = pl.pallas_call(
        functools.partial(bundle, count, width, halo),
        out_shape=arrays(far_sizes(count, blocks, halo)[-1], LANES),
        in_specs=[whole] * 5 + [any_place],
        out_specs=whole,
        compiler_params=grant(8),
        name="bundle",
    )(before, after, ahead_cells, behind_cells, thickness, force_tiles)
    far_pack = to_partner(pack)
    partner_3 = to_partner(after_all(sent_3, pack, partner_2))

    wall = jnp.stack([lax.axis_index("wall"), jnp.int32(walls)])
    own, own_force, own_partial, own_slopes, own_thick, inside = pl.pallas_call(
        functools.partial(own_part, planes, halo),
        out_shape=(arrays(blocks, tall, LANES),) * 3
        + (arrays(3 * blocks, tall, LANES),)
        + (arrays(depth, SUBLANES, LANES),) * 2,
        in_specs=[pl.BlockSpec(memory_space=pltpu.SMEM)] + [whole] * 7,
        out_specs=[whole] * 6,
        compiler_params=grant(14),
        name="own_part",
    )(wall, thickness, before, after, speed_tiles, force_tiles, ahead_cells, behind_cells)
    early = pl.pallas_call(
        functools.partial(before_force, planes, halo),
        out_shape=(arrays(blocks, tall, LANES),) * 4
        + (arrays(3 * blocks, tall, LANES), arrays(depth, SUBLANES, LANES))
        + (arrays(2 * depth, tall, LANES),) * 3,
        in_specs=[whole] * 8,
        out_specs=[whole] * 9,
        scratch_shapes=[rows],
        compiler_params=grant(20),
        name="before_force",
    )(partner_1, partner_2, far_pack, own, own_partial, own_slopes, own_thick, inside)
    out = pltpu.VMEM((count, width, cells), jnp.float32)
    speed_out, residual_out = pl.pallas_call(
        functools.partial(with_force, planes, halo),
        out_shape=(arrays(count, width, cells), arrays(count, width, cells)),
        in_specs=[whole] * 14,
        out_specs=[any_place] * 2,
        scratch_shapes=[out, out, pltpu.SemaphoreType.DMA((2, 3)), rows]
        + [pltpu.VMEM((depth, tall, LANES), jnp.float32)] * 3
        + [field] * 4
        + [slope],
        compiler_params=grant(30),
        name="with_force",
    )(partner_3, far_pack, own_force, own_thick, inside, *early)
    return speed_out.reshape(shape), residual_out.reshape(shape)


def local(starting_speed_vector, driving_source, viscosity):
    _, instants, planes, width, cells = starting_speed_vector.shape
    times = lax.axis_size("tm") * instants
    halo = 2 * ITERS
    one_instant = ITERS == 2 and instants == 1 and not instant_weights(times)
    tiled = planes * SUBLANES == LANES and cells == LANES and (width + 2 * halo) % SUBLANES == 0
    rows_fit = halo <= width and 3 * width <= LANES and (2 * halo) % SUBLANES == 0
    if one_instant and tiled and rows_fit:
        return carried(starting_speed_vector, driving_source, viscosity)
    return staged(starting_speed_vector, driving_source, viscosity)


def solution(mesh):
    placed = (P(None, "tm", None, "wall", "span"), P(None, "tm", None, "wall", "span"), P("wall"))
    return jax.shard_map(
        local,
        mesh=mesh,
        in_specs=placed,
        out_specs=(P(None, "tm", None, "wall", "span"), P(None, "tm", None, "wall", "span")),
        check_vma=False,
    )
```

```python
import functools

import jax
import jax.numpy as jnp
from jax import lax
from jax.experimental import pallas as pl
from jax.experimental.pallas import tpu as pltpu
from jax.sharding import PartitionSpec as P

ITERS = 2


step_rate = 0.05
LANES = 128
SUBLANES = 8
SIGNS = (1.0, -1.0, 1.0)


def instant_weights(instants):
    weights = {}
    for offset, weight in ((1, 0.5), (-1, -0.5)):
        weights[offset % instants] = weights.get(offset % instants, 0.0) + weight
    return {offset: weight for offset, weight in weights.items() if weight != 0.0}


def with_halo(cells, sides, width, closed):
    for axis, dim in sides:
        count = lax.axis_size(axis)
        ends = count if closed else count - 1
        head = lax.slice_in_dim(cells, 0, width, axis=dim)
        tail = lax.slice_in_dim(cells, cells.shape[dim] - width, cells.shape[dim], axis=dim)
        cells = jnp.concatenate(
            [
                lax.ppermute(tail, axis, [(i, (i + 1) % count) for i in range(ends)]),
                cells,
                lax.ppermute(head, axis, [((i + 1) % count, i) for i in range(ends)]),
            ],
            axis=dim,
        )
    return cells


def time_slope(values):
    instants = values.shape[1] * lax.axis_size("tm")
    if not instant_weights(instants):
        return jnp.zeros_like(values)
    padded_state = with_halo(values, (("tm", 1),), 1, True)
    return 0.5 * (padded_state[:, 2:] - padded_state[:, :-2])


def wall_pair(values):
    padded_state = with_halo(values, (("wall", 3),), 1, False)
    return (padded_state[:, :, :, 2:], padded_state[:, :, :, :-2])


def span_pair(values):
    padded_state = with_halo(values, (("span", 4),), 1, True)
    return (padded_state[:, :, :, :, 2:], padded_state[:, :, :, :, :-2])


def along_flow(values):
    return (jnp.roll(values, -1, 2), jnp.roll(values, 1, 2))


def partner_pairs():
    times, walls = lax.axis_size("tm"), lax.axis_size("wall")
    return [
        (time * walls + wall, ((time + times // 2) % times) * walls + walls - 1 - wall)
        for time in range(times)
        for wall in range(walls)
    ]


def reflect(values):
    sign_row = jnp.array(SIGNS, jnp.float32).reshape(3, 1, 1, 1, 1)
    partner = lax.ppermute(values, ("tm", "wall"), partner_pairs())
    return partner[:, :, :, ::-1, :] * sign_row


def residual_of(present_state, mirrored, driving_source, viscous):
    neighbours = (along_flow(present_state), wall_pair(present_state), span_pair(present_state))
    slopes = [0.5 * (ahead - behind) for ahead, behind in neighbours]
    advect = (
        present_state[0:1] * slopes[0]
        + present_state[1:2] * slopes[1]
        + present_state[2:3] * slopes[2]
    )
    laplace = neighbours[0][0] + neighbours[0][1] - 2.0 * present_state
    laplace = laplace + (neighbours[1][0] + neighbours[1][1] - 2.0 * present_state)
    laplace = laplace + (neighbours[2][0] + neighbours[2][1] - 2.0 * present_state)
    residual_now = (
        time_slope(present_state)
        + advect
        - viscous * laplace
        + 0.5 * (present_state - mirrored)
        - driving_source
    )
    return (residual_now, neighbours, slopes)


def descent_part(neighbours, slopes, residual_now, viscous):
    scaled = viscous * residual_now
    wall_ahead, wall_behind = wall_pair(jnp.concatenate((residual_now, scaled), 0))
    flow_ahead, flow_behind = along_flow(residual_now)
    span_ahead, span_behind = span_pair(residual_now)
    residual_pairs = (
        (flow_ahead, flow_behind),
        (wall_ahead[:3], wall_behind[:3]),
        (span_ahead, span_behind),
    )
    transport = jnp.stack(
        [jnp.sum(residual_now * slopes[component], axis=0) for component in range(3)]
    )
    second = None
    for axis_id in range(3):
        ahead_u = neighbours[axis_id][0][axis_id : axis_id + 1]
        behind_u = neighbours[axis_id][1][axis_id : axis_id + 1]
        term = 0.5 * (ahead_u * residual_pairs[axis_id][0] - behind_u * residual_pairs[axis_id][1])
        second = term if second is None else second + term
    diffused = viscous * flow_ahead + viscous * flow_behind - 2.0 * scaled
    diffused = diffused + (wall_ahead[3:] + wall_behind[3:] - 2.0 * scaled)
    diffused = diffused + (viscous * span_ahead + viscous * span_behind - 2.0 * scaled)
    return -time_slope(residual_now) + transport - second - diffused


def staged(starting_speed_vector, driving_source, viscosity):
    viscous = viscosity[None, None, None, :, None]
    present_state = starting_speed_vector
    residual_now = starting_speed_vector
    for iteration in range(ITERS):
        mirrored = reflect(present_state)
        residual_now, neighbours, slopes = residual_of(
            present_state, mirrored, driving_source, viscous
        )
        local_part = descent_part(neighbours, slopes, residual_now, viscous)
        mirror_residual = reflect(residual_now)
        present_state = present_state - step_rate * (
            local_part + 0.5 * (residual_now - mirror_residual)
        )
    return (present_state, residual_now)


GROUP = 17


def sweep(steps, step):
    rounds = steps // GROUP

    def several(index, carry):
        for inner in range(GROUP):
            step(pl.multiple_of((index * GROUP + inner + 1) * SUBLANES, SUBLANES))
        return carry

    if rounds > 1:
        lax.fori_loop(0, rounds, several, 0)
    done = rounds * GROUP if rounds > 1 else 0
    for index in range(done, steps):
        step((index + 1) * SUBLANES)


def edges(halo, speed_first, speed_last, force_first, force_last, thickness, own_first, own_last):
    count = speed_first.shape[0] // SUBLANES
    fields = ((speed_first, speed_last, halo), (force_first, force_last, halo - 1))
    at = 0
    for first, last, held in fields:
        for row in range(held):
            for plane in range(0, count, SUBLANES):
                start = plane * SUBLANES
                own_first[at : at + SUBLANES] = first[pl.ds(start + row, SUBLANES, stride=SUBLANES), :]
                own_last[at : at + SUBLANES] = last[pl.ds(start + SUBLANES - 1 - row, SUBLANES, stride=SUBLANES), :]
                at += SUBLANES
    spread = spread_of(thickness)
    own_first[at : at + SUBLANES] = spread
    own_last[at : at + SUBLANES] = spread


def spread_of(thickness):
    row = thickness[...]
    row = jnp.concatenate([row, jnp.zeros((1, LANES - row.shape[1]), jnp.float32)], axis=1)
    return jnp.broadcast_to(row, (SUBLANES, LANES))


def planes_of(*parts):
    return [part.at[plane] for part in parts for plane in range(part.shape[0])]


def extend_rows(rows, source, before, after, offset, held, halo, total=None, skip=0):
    count, width = len(source), source[0].shape[0]
    extended = width + 2 * halo
    for plane in range(count):
        rows[pl.ds(plane * extended + halo, width), :] = source[plane][...]
    for row in range(halo):
        for plane in range(0, count, SUBLANES):
            at = offset + row * (total or count) + skip + plane
            for edge, place in ((before, halo - 1 - row), (after, halo + width + row)):
                block = edge[pl.ds(at, SUBLANES), :] if row < held else jnp.zeros((SUBLANES, LANES), jnp.float32)
                rows[pl.ds(plane * extended + place, SUBLANES, stride=extended), :] = block


def to_tiles(rows, component, planes, tile, depth):
    extended = depth * SUBLANES
    blocks = [
        rows[pl.ds((component * planes + plane) * extended + tile, SUBLANES, stride=depth), :]
        for plane in range(planes)
    ]
    return jnp.concatenate(blocks, axis=0).T


def tile_fields(planes, halo, speed, force, before, after, rows):
    count, width, _ = speed.shape
    depth = (width + 2 * halo) // SUBLANES
    for part, (source, held, offset) in enumerate(((speed, halo, 0), (force, halo - 1, halo * count))):
        extend_rows(rows, planes_of(source), before, after, offset, held, halo)
        for component in range(3):
            for tile in range(depth):
                yield (part * 3 + component) * depth + tile, to_tiles(rows, component, planes, tile, depth)


def edge_cells(planes, halo, speed, force, before, after, _, first, last, rows):
    cells = speed.shape[-1]
    for place, block in tile_fields(planes, halo, speed, force, before, after, rows):
        first[place] = block[:halo]
        last[place] = block[cells - halo :]


def own_tiles(planes, halo, speed, force, before, after, _, speed_tiles, force_tiles, rows):
    blocks = speed_tiles.shape[0]
    for place, block in tile_fields(planes, halo, speed, force, before, after, rows):
        (speed_tiles if place < blocks else force_tiles)[place % blocks] = block


def far_sizes(count, blocks, halo):
    rows = (2 * halo - 3) * count
    cells = -(-(2 * halo - 3) * blocks // SUBLANES) * SUBLANES
    return (0, rows, 2 * rows, 2 * rows + cells, 2 * rows + 2 * cells, 2 * rows + 2 * cells + SUBLANES)


def bundle(count, width, halo, before, after, ahead_cells, behind_cells, thickness, _, pack):
    blocks = ahead_cells.shape[0] // 2
    starts = far_sizes(count, blocks, halo)
    speed_rows = (halo - 1) * count
    force_rows = (halo - 2) * count
    for source, start in ((before, starts[0]), (after, starts[1])):
        pack[start : start + speed_rows] = source[:speed_rows]
        pack[start + speed_rows : start + speed_rows + force_rows] = source[halo * count : halo * count + force_rows]
    for source, start, last in ((ahead_cells, starts[2], False), (behind_cells, starts[3], True)):
        at = start
        for part, held in ((0, halo - 1), (1, halo - 2)):
            for cell in range(held):
                from_edge = halo - 1 - cell if last else cell
                for place in range(blocks):
                    pack[at : at + 1] = source[part * blocks + place, from_edge : from_edge + 1]
                    at += 1
    held = before.shape[0] - SUBLANES
    lane = lax.broadcasted_iota(jnp.int32, (SUBLANES, LANES), 1)
    spread = spread_of(thickness)
    parts = jnp.where(lane < width, before[held : held + SUBLANES], pltpu.roll(spread, width, 1))
    parts = jnp.where(lane < 2 * width, parts, pltpu.roll(after[held : held + SUBLANES], 2 * width, 1))
    pack[starts[4] : starts[5]] = parts


def hold(*refs):
    pass


def turn(block):
    lanes = lax.broadcasted_iota(jnp.int32, block.shape, 1)
    return jnp.take_along_axis(block, lanes ^ (SUBLANES - 1), axis=1)


def wrap(field):
    ring = field.shape[1] - 2 * SUBLANES
    field[:, SUBLANES - 1 : SUBLANES] = field[:, SUBLANES + ring - 1 : SUBLANES + ring]
    field[:, SUBLANES + ring : SUBLANES + ring + 1] = field[:, SUBLANES : SUBLANES + 1]


def turned_tiles(field, source, pack, part, planes, halo, rows, components=range(3)):
    count = 3 * planes
    width, cells = source[0].shape
    depth = (width + 2 * halo) // SUBLANES
    blocks = 3 * depth
    starts = far_sizes(count, blocks, halo)
    held = halo - 1 - part
    before, after = pack.at[starts[0] : starts[1]], pack.at[starts[1] : starts[2]]
    extend_rows(rows, source, before, after, part * (halo - 1) * count, held, halo, count, components[0] * planes)
    offset = part * (halo - 1) * blocks
    for number, component in enumerate(components):
        for tile in range(depth):
            block = turn(to_tiles(rows, number, planes, tile, depth))
            place = number * depth + depth - 1 - tile
            field[place, SUBLANES : SUBLANES + cells] = -block if SIGNS[component] < 0 else block
    for start, end, base, way in (
        (starts[2], starts[3], SUBLANES + cells, 1),
        (starts[3], starts[4], SUBLANES + cells + 2 * halo - 1, -1),
    ):
        edge = turn(pack[start:end])
        for cell in range(halo):
            for number, component in enumerate(components):
                for tile in range(depth):
                    place = number * depth + depth - 1 - tile
                    at = offset + cell * blocks + component * depth + tile
                    line = edge[at : at + 1] if cell < held else jnp.zeros((1, LANES), jnp.float32)
                    field[place, base + way * cell : base + way * cell + 1] = -line if SIGNS[component] < 0 else line
    wrap(field)


class Joined:
    def __init__(self, *fields):
        self.rows = [(field, place) for field in fields for place in range(field.shape[0])]

    def __getitem__(self, at):
        field, place = self.rows[at[0]]
        return field[(place,) + at[1:]]


def close_far(far_open, far_force, own_open, inside, far_residual, own, first, steps):
    depth = inside.shape[0]

    def close(start):
        at = pl.ds(start, SUBLANES)
        for place in range(far_force.shape[0]):
            now = (far_open[first + place, at, :] - far_force[place, at, :]) * inside[place % depth]
            far_residual[place, at, :] = now
            own[place, at, :] = own_open[first + place, at, :] + (0.5 * step_rate) * now

    sweep(steps, close)
    wrap(far_residual)
    wrap(own)


def row_ahead(tiles, tile):
    return tiles[tile + 1] if tile + 1 < len(tiles) else pltpu.roll(tiles[0], LANES - 1, 1)


def row_behind(tiles, tile):
    return tiles[tile - 1] if tile > 0 else pltpu.roll(tiles[-1], 1, 1)


def plane_ahead(tile):
    return pltpu.roll(tile, LANES - SUBLANES, 1)


def plane_behind(tile):
    return pltpu.roll(tile, SUBLANES, 1)


def load(field, component, depth, start):
    return [field[component * depth + tile, pl.ds(start, SUBLANES), :] for tile in range(depth)]


def residual_stage(speed, mirrored, force, thick, inside, residual, slopes, steps):
    depth = thick.shape[0]

    def step(start):
        tiles = [load(speed, component, depth, start) for component in range(3)]
        for tile in range(depth):
            thin = thick[tile]
            middle = 6.0 * thin + 0.5
            half = [0.5 * tiles[component][tile] for component in range(3)]
            for component in range(3):
                place = component * depth + tile
                here = tiles[component][tile]
                pairs = (
                    (plane_ahead(here), plane_behind(here)),
                    (row_ahead(tiles[component], tile), row_behind(tiles[component], tile)),
                    (
                        speed[place, pl.ds(start + 1, SUBLANES), :],
                        speed[place, pl.ds(start - 1, SUBLANES), :],
                    ),
                )
                around = None
                total = None
                for axis_id, (ahead, behind) in enumerate(pairs):
                    slope = ahead - behind
                    if slopes is not None:
                        slopes[axis_id * 3 * depth + place, pl.ds(start, SUBLANES), :] = slope
                    both = ahead + behind
                    around = both if around is None else around + both
                    term = half[axis_id] * slope
                    total = term if total is None else total + term
                total = total - thin * around + middle * here
                if mirrored is not None:
                    total = total - 0.5 * mirrored[place, pl.ds(start, SUBLANES), :]
                if force is not None:
                    total = total - force[place, pl.ds(start, SUBLANES), :]
                if inside is not None:
                    total = total * inside[tile]
                residual[place, pl.ds(start, SUBLANES), :] = total

    sweep(steps, step)


def descent_stage(speed, residual, mirrored, thick, inside, slopes, following, steps):
    depth = thick.shape[0]

    def step(start):
        speeds = [load(speed, component, depth, start) for component in range(3)]
        tiles = [load(residual, component, depth, start) for component in range(3)]
        rises = []
        falls = []
        for tile in range(depth):
            half = 0.5 * speeds[1][tile]
            rises.append(half + thick[tile])
            falls.append(half - thick[tile])
        upper = [[rises[tile] * tiles[c][tile] for tile in range(depth)] for c in range(3)]
        lower = [[falls[tile] * tiles[c][tile] for tile in range(depth)] for c in range(3)]
        for tile in range(depth):
            thin = thick[tile]
            flow = 0.5 * speeds[0][tile]
            flow_rise, flow_fall = flow + thin, flow - thin
            span_rise = 0.5 * speed[2 * depth + tile, pl.ds(start + 1, SUBLANES), :] + thin
            span_fall = 0.5 * speed[2 * depth + tile, pl.ds(start - 1, SUBLANES), :] - thin
            half = [0.5 * tiles[component][tile] for component in range(3)]
            middle = 6.0 * thin + 0.5
            rate = step_rate * inside[tile]
            for component in range(3):
                place = component * depth + tile
                here = tiles[component][tile]
                total = middle * here
                for inner in range(3):
                    slope = slopes[
                        (component * 3 + inner) * depth + tile, pl.ds(start, SUBLANES), :
                    ]
                    total = total + half[inner] * slope
                total = total - plane_ahead(flow_rise * here) + plane_behind(flow_fall * here)
                total = total - row_ahead(upper[component], tile) + row_behind(lower[component], tile)
                total = total - span_rise * residual[place, pl.ds(start + 1, SUBLANES), :]
                total = total + span_fall * residual[place, pl.ds(start - 1, SUBLANES), :]
                if mirrored is not None:
                    total = total - 0.5 * mirrored[place, pl.ds(start, SUBLANES), :]
                following[place, pl.ds(start, SUBLANES), :] = speeds[component][tile] - rate * total

    sweep(steps, step)


def own_part(planes, halo, wall, thickness, before, after, speed_tiles, force_tiles, ahead_cells, behind_cells,
             own, own_force, own_open, own_slopes, own_thick, inside):
    count = 3 * planes
    width = thickness.shape[1]
    cells = speed_tiles.shape[1]
    depth = own_thick.shape[0]
    blocks = 3 * depth
    for part, (field, source) in enumerate(((own, speed_tiles), (own_force, force_tiles))):
        field[:, SUBLANES : SUBLANES + cells] = source[...]
        field[:, SUBLANES + cells : SUBLANES + cells + halo] = ahead_cells[part * blocks : part * blocks + blocks]
        field[:, SUBLANES + cells + halo : SUBLANES + cells + 2 * halo] = behind_cells[part * blocks : part * blocks + blocks]
    wrap(own)
    lane = lax.broadcasted_iota(jnp.int32, (SUBLANES, LANES), 1)
    held = before.shape[0] - SUBLANES
    spread = spread_of(thickness)
    own_spread = jnp.where(lane < width, before[held : held + SUBLANES], pltpu.roll(spread, width, 1))
    own_spread = jnp.where(lane < 2 * width, own_spread, pltpu.roll(after[held : held + SUBLANES], 2 * width, 1))
    for tile in range(depth):
        row = tile - halo + depth * (lane % SUBLANES)
        own_thick[tile] = jnp.take_along_axis(own_spread, width + row, axis=1)
        row = wall[0] * width + row
        inside[tile] = jnp.where((row >= 0) & (row < wall[1] * width), 1.0, 0.0).astype(jnp.float32)
    residual_stage(own, None, own_force, own_thick, None, own_open, own_slopes, (cells + 2 * halo) // SUBLANES)


def before_force(planes, halo, partner_1, partner_2, pack, own, own_partial, own_slopes, own_thick, inside,
                 far, own_residual, far_open, own_open, far_slopes, far_thick, far_force, far_residual, own_next,
                 rows):
    count = 3 * planes
    _, width, cells = partner_1.shape
    depth = own_thick.shape[0]
    blocks = 3 * depth
    lane = lax.broadcasted_iota(jnp.int32, (SUBLANES, LANES), 1)
    starts = far_sizes(count, blocks, halo)
    far_spread = pack[starts[4] : starts[5]]
    for tile in range(depth):
        row = tile - halo + depth * (lane % SUBLANES)
        far_thick[tile] = jnp.take_along_axis(far_spread, 2 * width - 1 - row, axis=1)
    turned_tiles(far, planes_of(partner_1), pack, 0, planes, halo, rows)
    steps = (cells + 2 * halo) // SUBLANES

    def close(start):
        at = pl.ds(start, SUBLANES)
        for place in range(blocks):
            own_residual[place, at, :] = (own_partial[place, at, :] - 0.5 * far[place, at, :]) * inside[place % depth]

    sweep(steps, close)
    wrap(own_residual)
    residual_stage(far, own, None, far_thick, None, far_open, far_slopes, steps)
    descent_stage(own, own_residual, None, own_thick, inside, own_slopes, own_open, steps)
    turned_tiles(far_force, planes_of(partner_2), pack, 1, planes, halo, rows, range(2))
    close_far(far_open, far_force, own_open, inside, far_residual, own_next, 0, steps)


def with_force(planes, halo, partner_last, pack,
               own_force, own_thick, inside, far, own_residual, far_open, own_open, far_slopes, far_thick,
               far_force_1, far_residual_1, own_1,
               speed_out, residual_out,
               speed_buffer, residual_buffer, sems, rows, far_force_2, far_residual_2, own_2,
               far_mirror, next_residual, next_own, next_far, own_slopes, partner_3, fetch_sems):
    _, width, cells = partner_3.shape
    share = partner_3.shape[0] // fetch_sems.shape[0]
    fetches = [
        pltpu.make_async_copy(
            partner_last.at[pl.ds(index * share, share)], partner_3.at[pl.ds(index * share, share)], fetch_sems.at[index]
        )
        for index in range(fetch_sems.shape[0])
    ]
    for fetch in fetches:
        fetch.start()
    for fetch in fetches:
        fetch.wait()
    depth = own_thick.shape[0]
    steps = (cells + 2 * halo) // SUBLANES
    turned_tiles(far_force_2, planes_of(partner_3), pack, 1, planes, halo, rows, range(2, 3))
    close_far(far_open, far_force_2, own_open, inside, far_residual_2, own_2, 2 * depth, steps)
    far_force = Joined(far_force_1, far_force_2)
    far_residual = Joined(far_residual_1, far_residual_2)
    own = Joined(own_1, own_2)
    descent_stage(far, far_residual, own_residual, far_thick, inside, far_slopes, next_far, steps)
    wrap(next_far)
    far = next_far
    residual_stage(own, far, own_force, own_thick, inside, next_residual, own_slopes, steps)
    wrap(next_residual)
    residual_copies = send_out(next_residual, residual_buffer, residual_out, sems.at[0], rows, planes, depth, halo)
    residual_stage(far, own, far_force, far_thick, inside, far_mirror, None, cells // SUBLANES)
    descent_stage(own, next_residual, far_mirror, own_thick, inside, own_slopes, next_own, cells // SUBLANES)
    speed_copies = send_out(next_own, speed_buffer, speed_out, sems.at[1], rows, planes, depth, halo)
    for copy in residual_copies + speed_copies:
        copy.wait()


def send_out(field, buffer, target, sems, rows, planes, depth, halo):
    _, width, cells = buffer.shape
    extended = depth * SUBLANES
    copies = []
    for component in range(3):
        for tile in range(depth):
            block = field[component * depth + tile, SUBLANES : SUBLANES + cells].T
            for plane in range(planes):
                at = (component * planes + plane) * extended + tile
                rows[pl.ds(at, SUBLANES, stride=depth), :] = block[plane * SUBLANES : (plane + 1) * SUBLANES]
        for plane in range(component * planes, (component + 1) * planes):
            buffer[plane] = rows[pl.ds(plane * extended + halo, width), :]
        part = pl.ds(component * planes, planes)
        copies.append(pltpu.make_async_copy(buffer.at[part], target.at[part], sems.at[component]))
        copies[-1].start()
    return copies


def carried(starting_speed_vector, driving_source, viscosity):
    shape = starting_speed_vector.shape
    _, _, planes, width, cells = shape
    halo = 2 * ITERS
    depth = (width + 2 * halo) // SUBLANES
    blocks = 3 * depth
    count = 3 * planes
    whole = pl.BlockSpec(memory_space=pltpu.VMEM)
    arrays = lambda *sizes: jax.ShapeDtypeStruct(sizes, jnp.float32)
    grant = lambda mega: pltpu.CompilerParams(vmem_limit_bytes=mega * 2**20)
    tall = cells + 2 * halo + 2 * SUBLANES
    rows = pltpu.VMEM((count * (width + 2 * halo), cells), jnp.float32)
    field = pltpu.VMEM((blocks, tall, LANES), jnp.float32)
    slope = pltpu.VMEM((3 * blocks, tall, LANES), jnp.float32)
    speed = starting_speed_vector.reshape(count, width, cells)
    force = driving_source.reshape(count, width, cells)

    walls, spans = lax.axis_size("wall"), lax.axis_size("span")
    upward = [(i, i + 1) for i in range(walls - 1)]
    downward = [(i + 1, i) for i in range(walls - 1)]
    onward = [(i, (i + 1) % spans) for i in range(spans)]
    backward = [((i + 1) % spans, i) for i in range(spans)]
    to_partner = functools.partial(lax.ppermute, axis_name=("tm", "wall"), perm=partner_pairs())

    cut = 2 * planes
    partner_1 = to_partner(speed)
    sent_2 = force[:cut]
    sent_3 = force[cut:]
    any_place = pl.BlockSpec(memory_space=pl.ANY)
    after_all = lambda held, *others: pl.pallas_call(
        hold,
        out_shape=arrays(*held.shape),
        in_specs=[any_place] * (1 + len(others)),
        out_specs=any_place,
        input_output_aliases={0: 0},
        compiler_params=grant(1),
        name="hold",
    )(held, *others)

    thickness = viscosity.reshape(1, width)
    tops = pl.BlockSpec((count, SUBLANES, cells), lambda i: (0, 0, 0))
    ends = pl.BlockSpec((count, SUBLANES, cells), lambda i: (0, width // SUBLANES - 1, 0))
    lines = (2 * halo - 1) * count + SUBLANES
    flat = lambda ref: ref.reshape(count * SUBLANES, cells)
    own_first, own_last = pl.pallas_call(
        lambda a, b, c, d, *rest: edges(halo, flat(a), flat(b), flat(c), flat(d), *rest),
        out_shape=(arrays(lines, cells),) * 2,
        grid=(1,),
        in_specs=[tops, ends, tops, ends, pl.BlockSpec((1, width), lambda i: (0, 0))],
        out_specs=[pl.BlockSpec((lines, cells), lambda i: (0, 0))] * 2,
        compiler_params=grant(8),
        name="edges",
    )(speed, speed, force, force, thickness)
    before = lax.ppermute(own_last, "wall", upward)
    after = lax.ppermute(own_first, "wall", downward)
    partner_2 = to_partner(after_all(sent_2, before, after))
    first, last = pl.pallas_call(
        functools.partial(edge_cells, planes, halo),
        out_shape=(arrays(2 * blocks, halo, LANES),) * 2,
        in_specs=[whole] * 4 + [any_place],
        out_specs=[whole] * 2,
        scratch_shapes=[rows],
        compiler_params=grant(8),
        name="edge_cells",
    )(speed, force, before, after, partner_1)
    speed_tiles, force_tiles = pl.pallas_call(
        functools.partial(own_tiles, planes, halo),
        out_shape=(arrays(blocks, cells, LANES),) * 2,
        in_specs=[whole] * 4 + [any_place],
        out_specs=[whole] * 2,
        scratch_shapes=[rows],
        compiler_params=grant(8),
        name="own_tiles",
    )(speed, force, before, after, first)
    behind_cells = lax.ppermute(last, "span", onward)
    ahead_cells = lax.ppermute(first, "span", backward)
    pack = pl.pallas_call(
        functools.partial(bundle, count, width, halo),
        out_shape=arrays(far_sizes(count, blocks, halo)[-1], LANES),
        in_specs=[whole] * 5 + [any_place],
        out_specs=whole,
        compiler_params=grant(8),
        name="bundle",
    )(before, after, ahead_cells, behind_cells, thickness, force_tiles)
    far_pack = to_partner(pack)
    partner_3 = to_partner(after_all(sent_3, pack, partner_2))

    wall = jnp.stack([lax.axis_index("wall"), jnp.int32(walls)])
    own, own_force, own_partial, own_slopes, own_thick, inside = pl.pallas_call(
        functools.partial(own_part, planes, halo),
        out_shape=(arrays(blocks, tall, LANES),) * 3
        + (arrays(3 * blocks, tall, LANES),)
        + (arrays(depth, SUBLANES, LANES),) * 2,
        in_specs=[pl.BlockSpec(memory_space=pltpu.SMEM)] + [whole] * 7,
        out_specs=[whole] * 6,
        compiler_params=grant(14),
        name="own_part",
    )(wall, thickness, before, after, speed_tiles, force_tiles, ahead_cells, behind_cells)
    early = pl.pallas_call(
        functools.partial(before_force, planes, halo),
        out_shape=(arrays(blocks, tall, LANES),) * 4
        + (arrays(3 * blocks, tall, LANES), arrays(depth, SUBLANES, LANES))
        + (arrays(2 * depth, tall, LANES),) * 3,
        in_specs=[whole] * 8,
        out_specs=[whole] * 9,
        scratch_shapes=[rows],
        compiler_params=grant(20),
        name="before_force",
    )(partner_1, partner_2, far_pack, own, own_partial, own_slopes, own_thick, inside)
    out = pltpu.VMEM((count, width, cells), jnp.float32)
    speed_out, residual_out = pl.pallas_call(
        functools.partial(with_force, planes, halo),
        out_shape=(arrays(count, width, cells), arrays(count, width, cells)),
        in_specs=[any_place] + [whole] * 13,
        out_specs=[any_place] * 2,
        scratch_shapes=[out, out, pltpu.SemaphoreType.DMA((2, 3)), rows]
        + [pltpu.VMEM((depth, tall, LANES), jnp.float32)] * 3
        + [field] * 4
        + [slope, pltpu.VMEM((count - cut, width, cells), jnp.float32), pltpu.SemaphoreType.DMA((8,))],
        compiler_params=grant(30),
        name="with_force",
    )(partner_3, far_pack, own_force, own_thick, inside, *early)
    return speed_out.reshape(shape), residual_out.reshape(shape)


def local(starting_speed_vector, driving_source, viscosity):
    _, instants, planes, width, cells = starting_speed_vector.shape
    times = lax.axis_size("tm") * instants
    halo = 2 * ITERS
    one_instant = ITERS == 2 and instants == 1 and not instant_weights(times)
    tiled = planes * SUBLANES == LANES and cells == LANES and (width + 2 * halo) % SUBLANES == 0
    rows_fit = halo <= width and 3 * width <= LANES and (2 * halo) % SUBLANES == 0
    if one_instant and tiled and rows_fit:
        return carried(starting_speed_vector, driving_source, viscosity)
    return staged(starting_speed_vector, driving_source, viscosity)


def solution(mesh):
    placed = (P(None, "tm", None, "wall", "span"), P(None, "tm", None, "wall", "span"), P("wall"))
    return jax.shard_map(
        local,
        mesh=mesh,
        in_specs=placed,
        out_specs=(P(None, "tm", None, "wall", "span"), P(None, "tm", None, "wall", "span")),
        check_vma=False,
    )
```
